128 devices in a mesh: dp: 16 (over x, z_hi, core), mp: 8 (over y, z_lo).
Axes of the slice: x: 4, y: 4, z: 4 (z_hi: 2, z_lo: 2; z = z_hi * 2 + z_lo), core: 2. Of those that a mesh axis runs over, the one named last changes fastest.
Arguments:
- hidden_rows: bfloat16 [64, 64, 5120], P('dp', None, 'mp')
- cotangent: bfloat16 [64, 64, 5120], P('dp', None, 'mp'), may hold values from -6 to 6
- lengths: int32 [64], P('dp'), may hold values from 1 to 63, as said below
- rewards: int32 [64], P('dp'), may hold values from -4 to 4
- swap_rows: int32 [16, 3, 2], P('dp'), may hold values from 0 to 3, as said below
- norm_gain: float32 [5120], P('mp'), may hold values from 0.5 to 2
- up_weight: bfloat16 [5120, 16384], P('mp', 'dp'), may hold values from -6 to 6
- down_weight: bfloat16 [16384, 5120], P('dp', 'mp'), may hold values from -6 to 6
Outputs:
- block_out: bfloat16 [64, 64, 5120], P('dp', None, 'mp')
- new_up: float32 [5120, 16384], P(None, ('dp', 'mp'))
- new_down: float32 [16384, 5120], P(('dp', 'mp'))
The draws below stay inside these ranges and needn't reach their ends.
Inputs may be any that keep to these rules, and one draw needn't show every extreme that they name: `swap_rows`: in every group and round the 2 listed slots are distinct. `lengths`: after the swaps of the first step, the rows of each group hold at most 128 live tokens together, and some group holds exactly 128.
All inputs are finite; a program needn't handle non-finite values.
Results may differ from the reference program's by a relative error of at most 0.0058.
Values may be sent and summed in bfloat16 or wider, within the bound.
A program may use at most 128 MiB of HBM per device.

```python
import math
import jax
import jax.numpy as jnp
from jax import lax

D = 5120
FF = 16384
ROWS_DEV = 4
SLOT = 64
ROUNDS = 3
HALF = 2
ROWS = 64
N_DP = 16


def swap_plan(key):
    key_order, key_first, key_second, key_full, key_shuffle = jax.random.split(jax.random.fold_in(key, 101), 5)
    scores = jax.random.randint(key_order, (N_DP, ROUNDS, ROWS_DEV), 0, 1 << 20)
    scores = scores * ROWS_DEV + jnp.arange(ROWS_DEV, dtype=jnp.int32)
    slot_table = jnp.argsort(scores, axis=-1, stable=True)[:, :, :HALF].astype(jnp.int32)
    full_group = jax.random.randint(key_full, (), 0, N_DP)
    is_full = (jnp.arange(N_DP, dtype=jnp.int32) == full_group)[:, None]
    first_pair = (jnp.arange(HALF, dtype=jnp.int32) == 0)[None, :]
    first_len = jax.random.randint(key_first, (N_DP, HALF), 1, SLOT)
    first_len = jnp.where(is_full & first_pair, SLOT - 1, first_len)
    second_len = jax.random.randint(key_second, (N_DP, HALF), 0, 1 << 20) % (SLOT - first_len) + 1
    second_len = jnp.where(is_full, SLOT - first_len, second_len)
    final_len = jnp.stack([first_len, second_len], axis=2).reshape(N_DP, ROWS_DEV)
    shuffle = jax.random.randint(key_shuffle, (N_DP, ROWS_DEV), 0, 1 << 20) * ROWS_DEV + jnp.arange(ROWS_DEV, dtype=jnp.int32)
    order = jnp.argsort(shuffle, axis=-1, stable=True)
    table = jnp.take_along_axis(final_len, order, axis=1)
    groups = jnp.arange(N_DP, dtype=jnp.int32)
    for round_index in (2, 1, 0):
        partner = jnp.bitwise_xor(groups, 1 << round_index)
        slot_list = slot_table[:, round_index, :]
        taken = table[partner[:, None], slot_list[partner]]
        table = table.at[groups[:, None], slot_list].set(taken)
    return (slot_table, table.reshape(ROWS).astype(jnp.int32))


def draw_swap_rows(key, part):
    slot_table, _ = swap_plan(key)
    return slot_table


def draw_lengths(key, part):
    _, length_list = swap_plan(key)
    return length_list


def draw_hidden_rows(key, part):
    key = jax.random.fold_in(key, 5)
    key_base, key_rough, key_rows = jax.random.split(key, 3)
    column = jnp.arange(D, dtype=jnp.float32) / D
    base = jax.random.normal(key_base, (ROWS, SLOT, D), jnp.float32)
    rise = jnp.exp(math.log(10.0) * (column - 0.5))
    spread = math.log(10.0)
    rough = jnp.exp(jax.random.uniform(key_rough, (D,), jnp.float32, -0.35, 0.35))
    row_scale = jnp.exp(jax.random.uniform(key_rows, (ROWS, SLOT, 1), jnp.float32, -0.5 * spread, 0.5 * spread))
    return (base * rise * rough * row_scale).astype(jnp.bfloat16)


def touch_ends(drawn, stream_key, least, top_value):
    extent = drawn.shape
    place = [jax.random.randint(jax.random.fold_in(stream_key, axis), (), 0, extent[axis]) for axis in range(len(extent))]
    drawn = drawn.at[tuple(place)].set(least)
    longest = extent.index(max(extent))
    place[longest] = (place[longest] + 1) % extent[longest]
    return drawn.at[tuple(place)].set(top_value)


def steps_of(key, extent, cuts, low, high):
    gain = 1.0
    for axis_at, parts in cuts:
        heights = jax.random.uniform(jax.random.fold_in(jax.random.fold_in(key, 6), axis_at), (parts,), jnp.float32, low / len(cuts), high / len(cuts))
        gain = gain * jnp.repeat(jnp.exp(heights), extent[axis_at] // parts).reshape((-1,) + (1,) * (len(extent) - 1 - axis_at))
    return gain


def normal_values(key, extent, deviation, most, cuts=(), kind=jnp.bfloat16):
    drawn = deviation * jax.random.normal(key, extent, jnp.float32)
    if cuts:
        drawn = drawn * steps_of(key, extent, cuts, -0.22, 0.18)
    return jnp.clip(drawn, -most, most).astype(kind)


def setup_inputs(seed: int = 0) -> dict:
    streams_of = jax.random.split(jax.random.key(seed), 9)
    return {
        "hidden_rows": draw_hidden_rows(jax.random.fold_in(streams_of[8], 71), 0),
        "cotangent": normal_values(streams_of[1], (ROWS, SLOT, D), 1.0, 6.0, ((0, 16), (2, 8))),
        "lengths": draw_lengths(jax.random.fold_in(streams_of[8], 71), 0),
        "rewards": touch_ends(jax.random.randint(streams_of[3], (ROWS,), -4, 5), jax.random.fold_in(streams_of[3], 1), -4, 4).astype(jnp.int32),
        "swap_rows": draw_swap_rows(jax.random.fold_in(streams_of[8], 71), 0),
        "norm_gain": jnp.clip(jnp.exp(math.log(2.0) - 1.3862944 * jax.random.uniform(streams_of[5], (D,), jnp.float32) ** steps_of(streams_of[5], (D,), ((0, 8),), -0.2, 0.2)), 0.5, 2.0),
        "up_weight": normal_values(streams_of[6], (D, FF), 1.0, 6.0, ((0, 8), (1, 16))),
        "down_weight": normal_values(streams_of[7], (FF, D), 1.0, 6.0, ((0, 16), (1, 8))),
    }


norm_eps = 1e-06
step_size = 4.0

def swap_round(source_table, slot_list, partner, groups):
    taken = source_table[partner[:, None], slot_list[partner]]
    return source_table.at[groups[:, None], slot_list].set(taken)

def unit_slope(preact):
    sigma = jax.nn.sigmoid(preact)
    return sigma * (1.0 + preact * (1.0 - sigma))

def reference(hidden_rows, cotangent, lengths, rewards, swap_rows, norm_gain, up_weight, down_weight):
    groups = jnp.arange(N_DP, dtype=jnp.int32)
    row_table = hidden_rows.reshape(N_DP, ROWS_DEV, SLOT, D)
    cot_table = cotangent.reshape(N_DP, ROWS_DEV, SLOT, D)
    length_table = lengths.reshape(N_DP, ROWS_DEV)
    reward_table = rewards.reshape(N_DP, ROWS_DEV)
    for round_index in range(ROUNDS):
        partner = jnp.bitwise_xor(groups, jnp.int32(1 << round_index)).astype(jnp.int32)
        slot_list = swap_rows[:, round_index, :].astype(jnp.int32)
        row_table = swap_round(row_table, slot_list, partner, groups)
        cot_table = swap_round(cot_table, slot_list, partner, groups)
        length_table = swap_round(length_table, slot_list, partner, groups)
        reward_table = swap_round(reward_table, slot_list, partner, groups)
    tokens_in = row_table.reshape(ROWS * SLOT, D)
    tokens_cot = cot_table.reshape(ROWS * SLOT, D)
    live = (jnp.arange(SLOT, dtype=jnp.int32)[None, None, :] < length_table[:, :, None]).reshape(-1)
    token_reward = jnp.repeat(reward_table.reshape(-1), SLOT).astype(jnp.float32) / 4.0
    as_float = tokens_in.astype(jnp.float32)
    mean_square = lax.optimization_barrier(jnp.mean(as_float * as_float, axis=1, keepdims=True))
    normed = (as_float * lax.rsqrt(mean_square + norm_eps) * norm_gain).astype(jnp.bfloat16)
    preact = jnp.dot(normed, up_weight, preferred_element_type=jnp.float32) / math.sqrt(D)
    hidden = jax.nn.silu(preact).astype(jnp.bfloat16)
    block = jnp.dot(hidden, down_weight, preferred_element_type=jnp.float32) / math.sqrt(FF)
    block_out = jnp.where(live[:, None], block, 0.0).astype(jnp.bfloat16).reshape(ROWS, SLOT, D)
    live_scale = jnp.where(live, token_reward, 0.0)
    out_grad = (tokens_cot.astype(jnp.float32) * live_scale[:, None]).astype(jnp.bfloat16)
    grad_down = jnp.dot(hidden.T, out_grad, preferred_element_type=jnp.float32) / math.sqrt(FF)
    grad_hidden = jnp.dot(out_grad, down_weight.T, preferred_element_type=jnp.float32) / math.sqrt(FF)
    grad_pre = (grad_hidden * unit_slope(preact)).astype(jnp.bfloat16)
    grad_up = jnp.dot(normed.T, grad_pre, preferred_element_type=jnp.float32) / math.sqrt(D)
    new_up = up_weight.astype(jnp.float32) - step_size * grad_up
    new_down = down_weight.astype(jnp.float32) - step_size * grad_down
    return (block_out, new_up, new_down)
```

```python
import math

import jax
import jax.numpy as jnp
from jax import lax
from jax.experimental import pallas as pl
from jax.experimental.pallas import tpu as pltpu
from jax.sharding import PartitionSpec as P

norm_eps = 1e-06
step_size = 4.0
MESH = pl.DeviceIdType.MESH

CAP = 128
ORDERS = (("x", "y", "z"), ("y", "z", "x"), ("z", "x", "y"))
PARTS = ((0, 48), (48, 48), (96, 32))
OFFSETS = (1, 3, 2)


def place():
    i = lax.axis_index("dp")
    j = lax.axis_index("mp")
    return {
        "x": i // 4,
        "y": j // 2,
        "z": ((i // 2) % 2) * 2 + j % 2,
        "c": i % 2,
    }


def device(at):
    z = at["z"]
    return ((at["x"] * 2 + z // 2) * 2 + at["c"], at["y"] * 2 + z % 2)


def shifted(at, axis, step):
    count = 2 if axis == "c" else 4
    return {**at, axis: (at[axis] + step) % count}


def spans(sel):
    def plain(s):
        if isinstance(s, tuple):
            return pl.ds(2 * s[1], 2)
        return pl.ds(0, 4) if s is None else pl.ds(s, 1)

    z = sel["z"]
    if z is None:
        z_lo, z_hi = pl.ds(0, 2), pl.ds(0, 2)
    elif isinstance(z, tuple):
        z_lo, z_hi = pl.ds(0, 2), pl.ds(z[1], 1)
    else:
        z_lo, z_hi = pl.ds(z % 2, 1), pl.ds(z // 2, 1)
    return (plain(sel["y"]), z_lo, plain(sel["x"]), z_hi)


def remote(src, dst, send, recv, at):
    return pltpu.make_async_remote_copy(
        src_ref=src,
        dst_ref=dst,
        send_sem=send,
        recv_sem=recv,
        device_id=device(at),
        device_id_type=MESH,
    )


def enter(peers):
    barrier = pltpu.get_barrier_semaphore()
    for at in peers:
        pl.semaphore_signal(barrier, inc=1, device_id=device(at), device_id_type=MESH)
    pl.semaphore_wait(barrier, len(peers))


def axis_peers(at):
    return [shifted(at, axis, k) for axis in "xyz" for k in OFFSETS]


def row_mask(meta, slot, slot_len):
    length = meta[slot, 0:1, 0:1]
    start = jnp.zeros((1, 1), jnp.int32)
    for before in range(slot):
        start = start + meta[before, 0:1, 0:1]
    token = lax.broadcasted_iota(jnp.int32, (CAP, slot_len), 0)
    spot = lax.broadcasted_iota(jnp.int32, (CAP, slot_len), 1)
    hit = jnp.logical_and(token == spot + start, spot < length)
    return jnp.where(hit, 1.0, 0.0).astype(jnp.bfloat16)


def gather_kernel(
    hid, cot, gain, lens, rew, swp, up, dn,
    g_norm, g_out, w_up, w_dn, meta_out,
    rows, out_rows, in_rows, meta, out_meta, in_meta, squares, packed,
    sq_send, sq_recv, swap_send, swap_recv, meta_send, meta_recv,
    up_send, up_recv, dn_send, dn_recv, local_sem, core_send, core_recv,
    s1_send, s1_recv, s2_send, s2_recv, s3_send, s3_recv,
):
    at = place()
    row_count, slot_len, width = hid.shape
    units = 128
    mp_peers = [
        shifted(shifted(at, "y", dy), "z", 0) if not dz else {**shifted(at, "y", dy), "z": (at["z"] // 2) * 2 + 1 - at["z"] % 2}
        for dy in range(4) for dz in range(2) if dy or dz
    ]
    diagonal = [p for n, p in enumerate(mp_peers) if n in (2, 4, 6)]
    core = shifted(at, "c", 1)
    enter(axis_peers(at) + diagonal + [core])

    flat = hid[...].reshape(row_count * slot_len, width).astype(jnp.float32)
    squares[7] = lax.dot_general(
        jnp.ones((8, width), jnp.float32), flat * flat, (((1,), (1,)), ((), ())),
        precision=lax.Precision.HIGHEST, preferred_element_type=jnp.float32,
    )
    sq_copies = []
    for n, peer in enumerate(mp_peers):
        copy = remote(squares.at[7], squares.at[n], sq_send.at[n], sq_recv.at[n], peer)
        copy.start()
        sq_copies.append(copy)

    for s in range(row_count):
        scale = rew[s].astype(jnp.float32) / 4.0
        rows[s, 1] = (cot[s].astype(jnp.float32) * scale).astype(jnp.bfloat16)
        meta[s] = jnp.full((8, 128), lens[s], jnp.int32)

    total = squares[7]
    for n, copy in enumerate(sq_copies):
        copy.wait()
        total = total + squares[n]
    factor = lax.rsqrt(total / (8 * width) + norm_eps)
    column = jnp.transpose(factor)[:, 0:1]
    normed = (flat * column * gain[...]).astype(jnp.bfloat16)
    for s in range(row_count):
        rows[s, 0] = normed[s * slot_len : (s + 1) * slot_len]

    j_me = at["y"] * 2 + at["z"] % 2
    own_units = pl.ds(pl.multiple_of(at["c"] * units, units), units)
    weight_copies = []
    for n, peer in enumerate(mp_peers):
        j_to = peer["y"] * 2 + peer["z"] % 2
        cut = pl.ds(pl.multiple_of(j_to * units, units), units)
        weight_copies.append(
            remote(up.at[:, cut], w_up.at[j_me, :, own_units], up_send.at[n], up_recv.at[n], peer)
        )
        weight_copies.append(
            remote(dn.at[cut], w_dn.at[j_me, own_units], dn_send.at[n], dn_recv.at[n], peer)
        )
    cut = pl.ds(pl.multiple_of(j_me * units, units), units)
    weight_copies.append(
        pltpu.make_async_copy(up.at[:, cut], w_up.at[j_me, :, own_units], local_sem.at[0])
    )
    weight_copies.append(
        pltpu.make_async_copy(dn.at[cut], w_dn.at[j_me, own_units], local_sem.at[1])
    )
    for copy in weight_copies:
        copy.start()

    partners = (core, shifted(at, "z", 2), {**at, "x": (at["x"] // 2) * 2 + 1 - at["x"] % 2})
    for r, peer in enumerate(partners):
        first, second = swp[r, 0], swp[r, 1]
        out_rows[r, 0] = rows[first]
        out_rows[r, 1] = rows[second]
        out_meta[r, 0] = meta[first]
        out_meta[r, 1] = meta[second]
        row_copy = remote(out_rows.at[r], in_rows.at[r], swap_send.at[r], swap_recv.at[r], peer)
        meta_copy = remote(out_meta.at[r], in_meta.at[r], meta_send.at[r], meta_recv.at[r], peer)
        meta_copy.start()
        row_copy.start()
        meta_copy.wait()
        row_copy.wait()
        for s in range(row_count):
            is_first, is_second = first == s, second == s
            rows[s] = jnp.where(is_first, in_rows[r, 0], jnp.where(is_second, in_rows[r, 1], rows[s]))
            meta[s] = jnp.where(is_first, in_meta[r, 0], jnp.where(is_second, in_meta[r, 1], meta[s]))
    meta_out[...] = meta[...]

    masks = [row_mask(meta, s, slot_len) for s in range(row_count)]
    for a in range(2):
        acc = jnp.zeros((CAP, width), jnp.float32)
        for s in range(row_count):
            acc = acc + jnp.dot(masks[s], rows[s, a], preferred_element_type=jnp.float32)
        packed[a, 0, 0, 0, 0] = acc.astype(jnp.bfloat16)

    here = spans({k: at[k] for k in "xyz"})
    bufs = (g_norm, g_out)
    own = []
    for a in range(2):
        copy = pltpu.make_async_copy(packed.at[a], bufs[a].at[here], local_sem.at[2 + a])
        copy.start()
        own.append(copy)
    first_copies = {}
    for a in range(2):
        for p, (r0, nr) in enumerate(PARTS):
            for k, step in enumerate(OFFSETS):
                row = pl.ds(r0, nr)
                copy = remote(
                    packed.at[a, :, :, :, :, row], bufs[a].at[here + (row,)],
                    s1_send.at[a, p, k], s1_recv.at[a, p, k], shifted(at, ORDERS[p][0], step),
                )
                copy.start()
                first_copies[a, p, k] = copy
    second_copies = {}
    for a in range(2):
        own[a].wait()
        for p, (r0, nr) in enumerate(PARTS):
            for k in range(3):
                first_copies[a, p, k].wait()
            one, two, three = ORDERS[p]
            piece = bufs[a].at[spans({one: None, two: at[two], three: at[three]}) + (pl.ds(r0, nr),)]
            for k, step in enumerate(OFFSETS):
                copy = remote(
                    piece, piece, s2_send.at[a, p, k], s2_recv.at[a, p, k], shifted(at, two, step)
                )
                copy.start()
                second_copies[a, p, k] = copy
    third_copies = {}
    for a in range(2):
        for p, (r0, nr) in enumerate(PARTS):
            for k in range(3):
                second_copies[a, p, k].wait()
            one, two, three = ORDERS[p]
            piece = bufs[a].at[spans({one: None, two: None, three: at[three]}) + (pl.ds(r0, nr),)]
            for k, step in enumerate((1, 3)):
                copy = remote(
                    piece, piece, s3_send.at[a, p, k], s3_recv.at[a, p, k], shifted(at, three, step)
                )
                copy.start()
                third_copies[a, p, k] = copy
    for copy in weight_copies:
        copy.wait()
    core_copies = []
    for n, (buf, where) in enumerate(((w_up, (slice(None), slice(None), own_units)), (w_dn, (slice(None), own_units)))):
        copy = remote(buf.at[where], buf.at[where], core_send.at[n], core_recv.at[n], core)
        copy.start()
        core_copies.append(copy)
    for a in range(2):
        for p, (r0, nr) in enumerate(PARTS):
            one, two, three = ORDERS[p]
            for k, step in enumerate((1, 3)):
                third_copies[a, p, k].wait()
                origin = (at[three] - step) % 4
                piece = bufs[a].at[spans({one: ("half", k), two: None, three: origin}) + (pl.ds(r0, nr),)]
                copy = remote(
                    piece, piece, s3_send.at[a, p, 2 + k], s3_recv.at[a, p, 2 + k], shifted(at, three, step)
                )
                copy.start()
                third_copies[a, p, 2 + k] = copy
    for a in range(2):
        for p in range(3):
            for k in range(2):
                third_copies[a, p, 2 + k].wait()
    for copy in core_copies:
        copy.wait()


def gather_all(hid, cot, gain, lens, rew, swp, up, dn):
    row_count, slot_len, width = hid.shape
    bf16 = jnp.bfloat16
    blocks = (4, 2, 4, 2, CAP, width)
    dma = pltpu.SemaphoreType.DMA
    vmem = pl.BlockSpec(memory_space=pltpu.VMEM)
    smem = pl.BlockSpec(memory_space=pltpu.SMEM)
    hbm = pl.BlockSpec(memory_space=pl.ANY)
    return pl.pallas_call(
        gather_kernel,
        out_shape=(
            jax.ShapeDtypeStruct(blocks, bf16),
            jax.ShapeDtypeStruct(blocks, bf16),
            jax.ShapeDtypeStruct((8, width, 256), bf16),
            jax.ShapeDtypeStruct((8, 256, width), bf16),
            jax.ShapeDtypeStruct((row_count, 8, 128), jnp.int32),
        ),
        in_specs=[vmem, vmem, vmem, smem, smem, smem, hbm, hbm],
        out_specs=(hbm, hbm, hbm, hbm, vmem),
        scratch_shapes=[
            pltpu.VMEM((row_count, 2, slot_len, width), bf16),
            pltpu.VMEM((3, 2, 2, slot_len, width), bf16),
            pltpu.VMEM((3, 2, 2, slot_len, width), bf16),
            pltpu.VMEM((row_count, 8, 128), jnp.int32),
            pltpu.VMEM((3, 2, 8, 128), jnp.int32),
            pltpu.VMEM((3, 2, 8, 128), jnp.int32),
            pltpu.VMEM((8, 8, row_count * slot_len), jnp.float32),
            pltpu.VMEM((2, 1, 1, 1, 1, CAP, width), bf16),
            dma((7,)), dma((7,)), dma((3,)), dma((3,)), dma((3,)), dma((3,)),
            dma((7,)), dma((7,)), dma((7,)), dma((7,)), dma((4,)), dma((2,)), dma((2,)),
            dma((2, 3, 3)), dma((2, 3, 3)), dma((2, 3, 3)), dma((2, 3, 3)),
            dma((2, 3, 4)), dma((2, 3, 4)),
        ],
        compiler_params=pltpu.CompilerParams(
            collective_id=1, has_side_effects=True, vmem_limit_bytes=32 << 20
        ),
        name="gather_all",
    )(hid, cot, gain, lens, rew, swp, up, dn)


def unit_slope(preact):
    sigma = 1.0 / (1.0 + jnp.exp(-preact))
    return sigma * (1.0 + preact * (1.0 - sigma))


def forward_kernel(root_width, g, w, preact, hidden, acc):
    j = pl.program_id(0)

    @pl.when(j == 0)
    def _():
        acc[...] = jnp.zeros_like(acc)

    acc[...] += jnp.dot(g[0], w[0], preferred_element_type=jnp.float32)

    @pl.when(j == 7)
    def _():
        value = acc[...] / root_width
        preact[...] = value
        hidden[...] = (value / (1.0 + jnp.exp(-value))).astype(jnp.bfloat16)


def middle_kernel(root_units, g, w, preact, hidden, block, grad_dn, grad_pre, acc):
    j = pl.program_id(0)
    c = lax.axis_index("dp") % 2

    @pl.when(j == 0)
    def _():
        acc[...] = jnp.zeros_like(acc)

    block[0] = jnp.dot(hidden[...], w[0], preferred_element_type=jnp.float32).astype(jnp.bfloat16)
    acc[...] += lax.dot_general(
        g[0], w[0], (((1,), (1,)), ((), ())), preferred_element_type=jnp.float32
    )
    grad = lax.dot_general(
        hidden[...], g[0], (((0,), (0,)), ((), ())), preferred_element_type=jnp.float32
    ) * (step_size / root_units)
    for h in range(2):
        base = jnp.where(c == h, w[0, h * 128 : (h + 1) * 128].astype(jnp.float32), 0.0)
        grad_dn[h] = base - grad[h * 128 : (h + 1) * 128]

    @pl.when(j == 7)
    def _():
        grad_pre[...] = (acc[...] / root_units * unit_slope(preact[...])).astype(jnp.bfloat16)


def up_kernel(root_width, g, w, grad_pre, grad_up):
    c = lax.axis_index("dp") % 2
    grad = lax.dot_general(
        g[0], grad_pre[...], (((0,), (0,)), ((), ())), preferred_element_type=jnp.float32
    ) * (step_size / root_width)
    for h in range(2):
        base = jnp.where(c == h, w[0, :, h * 128 : (h + 1) * 128].astype(jnp.float32), 0.0)
        grad_up[h] = base - grad[:, h * 128 : (h + 1) * 128]


def local_math(g_norm, g_out, w_up, w_dn, root_width, root_units):
    width = g_norm.shape[-1]
    tokens = 8 * CAP
    g_norm = g_norm.reshape(8, tokens, width)
    g_out = g_out.reshape(8, tokens, width)
    f32, bf16 = jnp.float32, jnp.bfloat16
    g_spec = pl.BlockSpec((1, tokens, width), lambda j: (j, 0, 0))
    wu_spec = pl.BlockSpec((1, width, 256), lambda j: (j, 0, 0))
    wd_spec = pl.BlockSpec((1, 256, width), lambda j: (j, 0, 0))
    whole = pl.BlockSpec((tokens, 256), lambda j: (0, 0))
    params = pltpu.CompilerParams(vmem_limit_bytes=48 << 20)

    def bind(fn, *args):
        return lambda *refs: fn(*args, *refs)

    preact, hidden = pl.pallas_call(
        bind(forward_kernel, root_width),
        grid=(8,),
        in_specs=[g_spec, wu_spec],
        out_specs=(whole, whole),
        out_shape=(
            jax.ShapeDtypeStruct((tokens, 256), f32),
            jax.ShapeDtypeStruct((tokens, 256), bf16),
        ),
        scratch_shapes=[pltpu.VMEM((tokens, 256), f32)],
        compiler_params=params,
        name="forward",
    )(g_norm, w_up)
    block, grad_dn, grad_pre = pl.pallas_call(
        bind(middle_kernel, root_units),
        grid=(8,),
        in_specs=[g_spec, wd_spec, whole, whole],
        out_specs=(
            g_spec,
            pl.BlockSpec((2, 128, width), lambda j: (0, 0, j)),
            whole,
        ),
        out_shape=(
            jax.ShapeDtypeStruct((8, tokens, width), bf16),
            jax.ShapeDtypeStruct((2, 128, 8 * width), f32),
            jax.ShapeDtypeStruct((tokens, 256), bf16),
        ),
        scratch_shapes=[pltpu.VMEM((tokens, 256), f32)],
        compiler_params=params,
        name="middle",
    )(g_out, w_dn, preact, hidden)
    grad_up = pl.pallas_call(
        bind(up_kernel, root_width),
        grid=(8,),
        in_specs=[g_spec, wu_spec, whole],
        out_specs=pl.BlockSpec((2, width, 128), lambda j: (0, j, 0)),
        out_shape=jax.ShapeDtypeStruct((2, 8 * width, 128), f32),
        compiler_params=params,
        name="up_grad",
    )(g_norm, w_up, grad_pre)
    return block.reshape(4, 2, 4, 2, CAP, width), grad_dn, grad_up


def sizes(sel, nr, width):
    def plain(s):
        return 2 if isinstance(s, tuple) else (4 if s is None else 1)

    z = sel["z"]
    z_dims = (2, 2) if z is None else ((2, 1) if isinstance(z, tuple) else (1, 1))
    return (plain(sel["y"]), z_dims[0], plain(sel["x"]), z_dims[1], nr, width)


def lead(q, dims):
    d = q % dims[3]
    q = q // dims[3]
    c = q % dims[2]
    q = q // dims[2]
    b = q % dims[1]
    return (q // dims[1], b, c, d)


def scatter_kernel(root_units, part, meta, out, *refs):
    at = place()
    row_count, slot_len, width = out.shape
    half_bufs, full_bufs, two_bufs, one_bufs = refs[0:3], refs[3:6], refs[6:9], refs[9:12]
    tokens = refs[12]
    h_send, h_recv, f_send, f_recv, t_send, t_recv, o_send, o_recv = refs[13:]
    enter(axis_peers(at))
    count = lambda dims: dims[0] * dims[1] * dims[2] * dims[3]

    sends = {}
    for p, (r0, nr) in enumerate(PARTS):
        one, two, three = ORDERS[p]
        row = pl.ds(r0, nr)
        for k, step in enumerate((1, 3)):
            src = part.at[spans({one: (at[one] + 2) % 4, two: ("half", k), three: None}) + (row,)]
            sends[p, k] = remote(
                src, half_bufs[p].at[k], h_send.at[p, k], h_recv.at[p, k], shifted(at, one, step)
            )
            sends[p, k].start()
        for k, step in enumerate((1, 3)):
            other = 1 - k
            src = part.at[spans({one: (at[one] + step) % 4, two: ("half", other), three: None}) + (row,)]
            dst = full_bufs[p].at[(k,) + spans({one: 0, two: ("half", other), three: None})]
            sends[p, 2 + k] = remote(
                src, dst, f_send.at[p, k, 0], f_recv.at[p, k, 0], shifted(at, one, step)
            )
            sends[p, 2 + k].start()
    for p, (r0, nr) in enumerate(PARTS):
        one, two, three = ORDERS[p]
        for k, step in enumerate((1, 3)):
            sends[p, k].wait()
            sel = {one: 0, two: ("half", k), three: None}
            dims = sizes(sel, nr, width)[:4]
            base = {one: (at[one] + step) % 4, two: ("half", k), three: None}
            starts = [s.start for s in spans(base)]

            def add(q, carry, p=p, k=k, dims=dims, starts=starts, r0=r0, nr=nr):
                ix = lead(q, dims)
                there = tuple(s + i for s, i in zip(starts, ix))
                half_bufs[p][(k,) + ix] = half_bufs[p][(k,) + ix] + part[there + (pl.ds(r0, nr),)]
                return carry

            lax.fori_loop(0, count(dims), add, 0)
            dst = full_bufs[p].at[(k,) + spans(sel)]
            sends[p, 4 + k] = remote(
                half_bufs[p].at[k], dst, f_send.at[p, k, 1], f_recv.at[p, k, 1], shifted(at, one, step)
            )
            sends[p, 4 + k].start()
    for p, (r0, nr) in enumerate(PARTS):
        one, two, three = ORDERS[p]
        for n in (2, 3, 4, 5):
            sends[p, n].wait()
        dims = sizes({one: 0, two: None, three: None}, nr, width)[:4]
        starts = [s.start for s in spans({one: at[one], two: None, three: None})]

        def add(q, carry, p=p, dims=dims, starts=starts, r0=r0, nr=nr):
            ix = lead(q, dims)
            there = tuple(s + i for s, i in zip(starts, ix))
            value = full_bufs[p][(0,) + ix].astype(jnp.float32) + full_bufs[p][(1,) + ix].astype(jnp.float32)
            value = value + part[there + (pl.ds(r0, nr),)].astype(jnp.float32)
            full_bufs[p][(0,) + ix] = value.astype(jnp.bfloat16)
            return carry

        lax.fori_loop(0, count(dims), add, 0)
        for k, step in enumerate(OFFSETS):
            src = full_bufs[p].at[(0,) + spans({one: 0, two: (at[two] + step) % 4, three: None})]
            sends[p, 6 + k] = remote(
                src, two_bufs[p].at[k], t_send.at[p, k], t_recv.at[p, k], shifted(at, two, step)
            )
            sends[p, 6 + k].start()
    for p, (r0, nr) in enumerate(PARTS):
        one, two, three = ORDERS[p]
        for k in range(3):
            sends[p, 6 + k].wait()
        dims = sizes({one: 0, two: 0, three: None}, nr, width)[:4]
        starts = [s.start for s in spans({one: 0, two: at[two], three: None})]
        for q in range(4):
            ix = lead(q, dims)
            there = tuple(s + i for s, i in zip(starts, ix))
            value = full_bufs[p][(0,) + there].astype(jnp.float32)
            for k in range(3):
                value = value + two_bufs[p][(k,) + ix].astype(jnp.float32)
            two_bufs[p][(0,) + ix] = value.astype(jnp.bfloat16)
        for k, step in enumerate(OFFSETS):
            src = two_bufs[p].at[(0,) + spans({one: 0, two: 0, three: (at[three] + step) % 4})]
            sends[p, 9 + k] = remote(
                src, one_bufs[p].at[k], o_send.at[p, k], o_recv.at[p, k], shifted(at, three, step)
            )
            sends[p, 9 + k].start()
    for p, (r0, nr) in enumerate(PARTS):
        one, two, three = ORDERS[p]
        for k in range(3):
            sends[p, 9 + k].wait()
        there = tuple(s.start for s in spans({one: 0, two: 0, three: at[three]}))
        value = two_bufs[p][(0,) + there].astype(jnp.float32)
        for k in range(3):
            value = value + one_bufs[p][k, 0, 0, 0, 0].astype(jnp.float32)
        tokens[pl.ds(r0, nr)] = (value / root_units).astype(jnp.bfloat16)
    for s in range(row_count):
        out[s] = lax.dot_general(
            row_mask(meta, s, slot_len), tokens[...], (((0,), (0,)), ((), ())),
            preferred_element_type=jnp.float32,
        ).astype(jnp.bfloat16)


def scatter_all(part, meta, slot_len, root_units):
    width = part.shape[-1]
    row_count = meta.shape[0]
    bf16 = jnp.bfloat16
    dma = pltpu.SemaphoreType.DMA
    vmem = pl.BlockSpec(memory_space=pltpu.VMEM)
    half, full, two_b, one_b = [], [], [], []
    for (one, two, three), (_, nr) in zip(ORDERS, PARTS):
        half.append(pltpu.VMEM((2,) + sizes({one: 0, two: ("half", 0), three: None}, nr, width), bf16))
        full.append(pltpu.VMEM((2,) + sizes({one: 0, two: None, three: None}, nr, width), bf16))
        two_b.append(pltpu.VMEM((3,) + sizes({one: 0, two: 0, three: None}, nr, width), bf16))
        one_b.append(pltpu.VMEM((3, 1, 1, 1, 1, nr, width), bf16))

    def body(*refs):
        scatter_kernel(root_units, *refs)

    return pl.pallas_call(
        body,
        out_shape=jax.ShapeDtypeStruct((row_count, slot_len, width), bf16),
        in_specs=[vmem, vmem],
        out_specs=vmem,
        scratch_shapes=half + full + two_b + one_b + [
            pltpu.VMEM((CAP, width), bf16),
            dma((3, 2)), dma((3, 2)), dma((3, 2, 2)), dma((3, 2, 2)),
            dma((3, 3)), dma((3, 3)), dma((3, 3)), dma((3, 3)),
        ],
        compiler_params=pltpu.CompilerParams(
            collective_id=2, has_side_effects=True, vmem_limit_bytes=48 << 20
        ),
        name="scatter_all",
    )(part, meta)


def on_device(
    hidden_rows, cotangent, lengths, rewards, swap_rows, norm_gain, up_weight, down_weight
):
    row_count, slot_len, width = hidden_rows.shape
    root_width = math.sqrt(width * lax.axis_size("mp"))
    root_units = math.sqrt(up_weight.shape[1] * lax.axis_size("dp"))
    g_norm, g_out, w_up, w_dn, meta = gather_all(
        hidden_rows, cotangent, norm_gain.reshape(1, width), lengths, rewards,
        swap_rows.reshape(3, 2), up_weight, down_weight,
    )
    part, grad_dn, grad_up = local_math(g_norm, g_out, w_up, w_dn, root_width, root_units)
    c = lax.axis_index("dp") % 2
    pairs = [(i, i ^ 1) for i in range(lax.axis_size("dp"))]
    new = []
    for both in (grad_up, grad_dn):
        mine = lax.dynamic_index_in_dim(both, c, 0, keepdims=False)
        other = lax.dynamic_index_in_dim(both, 1 - c, 0, keepdims=False)
        new.append(mine + lax.ppermute(other, "dp", pairs))
    block_out = scatter_all(part, meta, slot_len, root_units)
    return (block_out, new[0], new[1])


def solution(mesh):
    return jax.shard_map(
        on_device,
        mesh=mesh,
        in_specs=(
            P("dp", None, "mp"),
            P("dp", None, "mp"),
            P("dp"),
            P("dp"),
            P("dp", None, None),
            P("mp"),
            P("mp", "dp"),
            P("dp", "mp"),
        ),
        out_specs=(P("dp", None, "mp"), P(None, ("dp", "mp")), P(("dp", "mp"), None)),
        check_vma=False,
    )
```

```python
import math

import jax
import jax.numpy as jnp
from jax import lax
from jax.experimental import pallas as pl
from jax.experimental.pallas import tpu as pltpu
from jax.sharding import PartitionSpec as P

norm_eps = 1e-06
step_size = 4.0
MESH = pl.DeviceIdType.MESH

CAP = 128
ORDERS = (("x", "y", "z"), ("y", "z", "x"), ("z", "x", "y"))
PARTS = (
    ((0, 48), (48, 48), (96, 32)),
    ((0, 32), (32, 48), (80, 48)),
    ((0, 32), (32, 48), (80, 48)),
)
OFFSETS = (1, 3, 2)


def place():
    i = lax.axis_index("dp")
    j = lax.axis_index("mp")
    return {
        "x": i // 4,
        "y": j // 2,
        "z": ((i // 2) % 2) * 2 + j % 2,
        "c": i % 2,
    }


def device(at):
    z = at["z"]
    return ((at["x"] * 2 + z // 2) * 2 + at["c"], at["y"] * 2 + z % 2)


def shifted(at, axis, step):
    count = 2 if axis == "c" else 4
    return {**at, axis: (at[axis] + step) % count}


def spans(sel):
    def plain(s):
        if isinstance(s, tuple):
            return pl.ds(2 * s[1], 2)
        return pl.ds(0, 4) if s is None else pl.ds(s, 1)

    z = sel["z"]
    if z is None:
        z_lo, z_hi = pl.ds(0, 2), pl.ds(0, 2)
    elif isinstance(z, tuple):
        z_lo, z_hi = pl.ds(0, 2), pl.ds(z[1], 1)
    else:
        z_lo, z_hi = pl.ds(z % 2, 1), pl.ds(z // 2, 1)
    return (plain(sel["y"]), z_lo, plain(sel["x"]), z_hi)


def remote(src, dst, send, recv, at):
    return pltpu.make_async_remote_copy(
        src_ref=src,
        dst_ref=dst,
        send_sem=send,
        recv_sem=recv,
        device_id=device(at),
        device_id_type=MESH,
    )


def enter(peers):
    barrier = pltpu.get_barrier_semaphore()
    for at in peers:
        pl.semaphore_signal(barrier, inc=1, device_id=device(at), device_id_type=MESH)
    pl.semaphore_wait(barrier, len(peers))


def axis_peers(at):
    return [shifted(at, axis, k) for axis in "xyz" for k in OFFSETS]


def row_mask(meta, slot, slot_len):
    length = meta[slot, 0:1, 0:1]
    start = jnp.zeros((1, 1), jnp.float32)
    for before in range(slot):
        start = start + meta[before, 0:1, 0:1]
    token = lax.broadcasted_iota(jnp.int32, (CAP, slot_len), 0).astype(jnp.float32)
    spot = lax.broadcasted_iota(jnp.int32, (CAP, slot_len), 1).astype(jnp.float32)
    return jnp.logical_and(token == spot + start, spot < length)


def sizes(sel, nr, width):
    def plain(s):
        return 2 if isinstance(s, tuple) else (4 if s is None else 1)

    z = sel["z"]
    z_dims = (2, 2) if z is None else ((2, 1) if isinstance(z, tuple) else (1, 1))
    return (plain(sel["y"]), z_dims[0], plain(sel["x"]), z_dims[1], nr, width)


def lead(q, dims):
    d = q % dims[3]
    q = q // dims[3]
    c = q % dims[2]
    q = q // dims[2]
    b = q % dims[1]
    return (q // dims[1], b, c, d)


def starts_of(sel):
    return tuple(s.start for s in spans(sel))


def moved(base, ix):
    return tuple(s + i for s, i in zip(base, ix))


def count(dims):
    return dims[0] * dims[1] * dims[2] * dims[3]


def unit_slope(preact):
    sigma = 1.0 / (1.0 + jnp.exp(-preact))
    return sigma * (1.0 + preact * (1.0 - sigma))


def step_kernel(
    root_width, root_units,
    hid, cot, gain, lens, rew, swp, up, dn,
    out, new_up, new_dn, g_norm, g_out,
    h_rows, c_rows, out_rows, in_rows, meta, out_meta, in_meta, squares, packed, masks,
    w_up, w_dn, stream, acc, hidden, turned, slope, part,
    own_up, oth_up, got_up, own_dn, oth_dn, got_dn, tokens,
    half_0, half_1, half_2, full_0, full_1, full_2,
    two_0, two_1, two_2, one_0, one_1, one_2,
    sq_send, sq_recv, swap_send, swap_recv, meta_send, meta_recv,
    up_send, up_recv, dn_send, dn_recv, local_sem, core_send, core_recv,
    s1_send, s1_recv, s2_send, s2_recv, s3_send, s3_recv,
    stream_sem, gu_send, gu_recv, gd_send, gd_recv, nu_sem, nd_sem,
    h_send, h_recv, f_send, f_recv, t_send, t_recv, o_send, o_recv,
):
    at = place()
    row_count, slot_len, width = hid.shape
    units = 128
    f32, bf16 = jnp.float32, jnp.bfloat16
    half_bufs, full_bufs = (half_0, half_1, half_2), (full_0, full_1, full_2)
    two_bufs, one_bufs = (two_0, two_1, two_2), (one_0, one_1, one_2)

    load_h = pltpu.make_async_copy(hid, h_rows, local_sem.at[4])
    load_c = pltpu.make_async_copy(cot, c_rows, local_sem.at[5])
    load_h.start()
    load_c.start()
    mp_peers = [
        {**shifted(at, "y", dy), "z": (at["z"] // 2) * 2 + (at["z"] % 2 + dz) % 2}
        for dy in range(4) for dz in range(2) if dy or dz
    ]
    diagonal = [p for n, p in enumerate(mp_peers) if n in (2, 4, 6)]
    core = shifted(at, "c", 1)
    enter(axis_peers(at) + diagonal + [core])
    partners = (core, shifted(at, "z", 2), {**at, "x": (at["x"] // 2) * 2 + 1 - at["x"] % 2})

    store = (h_rows, c_rows)

    def swap_start(r, a):
        out_rows[r, a, 0] = store[a][swp[0, r, 0]]
        out_rows[r, a, 1] = store[a][swp[0, r, 1]]
        copy = remote(
            out_rows.at[r, a], in_rows.at[r, a], swap_send.at[r, a], swap_recv.at[r, a], partners[r]
        )
        copy.start()
        return copy

    def swap_end(r, a, copy):
        copy.wait()
        first, second = swp[0, r, 0], swp[0, r, 1]
        for s in range(row_count):
            store[a][s] = jnp.where(
                first == s, in_rows[r, a, 0], jnp.where(second == s, in_rows[r, a, 1], store[a][s])
            )

    def meta_start(r):
        out_meta[r, 0] = meta[swp[0, r, 0]]
        out_meta[r, 1] = meta[swp[0, r, 1]]
        copy = remote(out_meta.at[r], in_meta.at[r], meta_send.at[r], meta_recv.at[r], partners[r])
        copy.start()
        return copy

    def meta_end(r, copy):
        copy.wait()
        first, second = swp[0, r, 0], swp[0, r, 1]
        for s in range(row_count):
            meta[s] = jnp.where(first == s, in_meta[r, 0], jnp.where(second == s, in_meta[r, 1], meta[s]))

    load_h.wait()
    move_h = swap_start(0, 0)
    flat = hid_value = h_rows[...].reshape(row_count * slot_len, width).astype(f32)
    squares[7] = lax.dot_general(
        jnp.ones((8, width), f32), flat * hid_value, (((1,), (1,)), ((), ())),
        precision=lax.Precision.HIGHEST, preferred_element_type=f32,
    )
    sq_copies = []
    for n, peer in enumerate(mp_peers):
        copy = remote(squares.at[7], squares.at[n], sq_send.at[n], sq_recv.at[n], peer)
        copy.start()
        sq_copies.append(copy)
    load_c.wait()
    move_c = swap_start(0, 1)
    swap_end(0, 0, move_h)
    move_h = swap_start(1, 0)
    total = squares[7]
    for n, copy in enumerate(sq_copies):
        copy.wait()
        total = total + squares[n]
    factor = lax.rsqrt(total / (8 * width) + norm_eps)
    for s in range(row_count):
        meta[s, 0:1] = jnp.full((1, 128), lens[s].astype(f32), f32)
        meta[s, 1:2] = jnp.full((1, 128), rew[s].astype(f32), f32)
        meta[s, 2:8] = jnp.zeros((6, 128), f32)
        meta[s, 2:3, 0:slot_len] = factor[0:1, s * slot_len : (s + 1) * slot_len]
    move_m = meta_start(0)
    swap_end(0, 1, move_c)
    move_c = swap_start(1, 1)
    meta_end(0, move_m)
    move_m = meta_start(1)

    j_me = at["y"] * 2 + at["z"] % 2
    own_units = pl.ds(pl.multiple_of(at["c"] * units, units), units)
    weight_copies = []
    for n, peer in enumerate(mp_peers):
        j_to = peer["y"] * 2 + peer["z"] % 2
        cut = pl.ds(pl.multiple_of(j_to * units, units), units)
        weight_copies.append(
            remote(up.at[:, cut], w_up.at[j_me, :, own_units], up_send.at[n], up_recv.at[n], peer)
        )
        weight_copies.append(
            remote(dn.at[cut], w_dn.at[j_me, own_units], dn_send.at[n], dn_recv.at[n], peer)
        )
    cut = pl.ds(pl.multiple_of(j_me * units, units), units)
    weight_copies.append(
        pltpu.make_async_copy(up.at[:, cut], w_up.at[j_me, :, own_units], local_sem.at[0])
    )
    weight_copies.append(
        pltpu.make_async_copy(dn.at[cut], w_dn.at[j_me, own_units], local_sem.at[1])
    )
    for copy in weight_copies:
        copy.start()

    swap_end(1, 0, move_h)
    move_h = swap_start(2, 0)
    swap_end(1, 1, move_c)
    move_c = swap_start(2, 1)
    meta_end(1, move_m)
    move_m = meta_start(2)
    meta_end(2, move_m)
    norm_scale = jnp.zeros((CAP, 1), f32)
    grad_scale = jnp.zeros((CAP, 1), f32)
    for s in range(row_count):
        hit = row_mask(meta, s, slot_len)
        masks[s] = jnp.where(hit, 1.0, 0.0).astype(bf16)
        norm_scale += jnp.sum(jnp.where(hit, meta[s, 2:3, 0:slot_len], 0.0), axis=1, keepdims=True)
        grad_scale += jnp.sum(jnp.where(hit, meta[s, 1:2, 0:slot_len], 0.0), axis=1, keepdims=True)

    def pack(a):
        picked = jnp.zeros((CAP, width), f32)
        for s in range(row_count):
            picked = picked + jnp.dot(masks[s], store[a][s], preferred_element_type=f32)
        return picked

    here = spans({k: at[k] for k in "xyz"})
    bufs = (g_norm, g_out)
    own, first_copies, second_copies, third_copies = [], {}, {}, {}

    def gather_first(a):
        copy = pltpu.make_async_copy(packed.at[a], bufs[a].at[here], local_sem.at[2 + a])
        copy.start()
        own.append(copy)
        for p, (r0, nr) in enumerate(PARTS[a]):
            for k, step in enumerate(OFFSETS):
                row = pl.ds(r0, nr)
                copy = remote(
                    packed.at[a, :, :, :, :, row], bufs[a].at[here + (row,)],
                    s1_send.at[a, p, k], s1_recv.at[a, p, k], shifted(at, ORDERS[p][0], step),
                )
                copy.start()
                first_copies[a, p, k] = copy

    def gather_second(a):
        own[a].wait()
        for p, (r0, nr) in enumerate(PARTS[a]):
            for k in range(3):
                first_copies[a, p, k].wait()
            one, two, three = ORDERS[p]
            piece = bufs[a].at[spans({one: None, two: at[two], three: at[three]}) + (pl.ds(r0, nr),)]
            for k, step in enumerate(OFFSETS):
                copy = remote(
                    piece, piece, s2_send.at[a, p, k], s2_recv.at[a, p, k], shifted(at, two, step)
                )
                copy.start()
                second_copies[a, p, k] = copy

    def gather_third(a, p):
        r0, nr = PARTS[a][p]
        for k in range(3):
            second_copies[a, p, k].wait()
        one, two, three = ORDERS[p]
        piece = bufs[a].at[spans({one: None, two: None, three: at[three]}) + (pl.ds(r0, nr),)]
        for k, step in enumerate((1, 3)):
            copy = remote(
                piece, piece, s3_send.at[a, p, k], s3_recv.at[a, p, k], shifted(at, three, step)
            )
            copy.start()
            third_copies[a, p, k] = copy

    def gather_pass_on(a, p):
        r0, nr = PARTS[a][p]
        one, two, three = ORDERS[p]
        for k, step in enumerate((1, 3)):
            third_copies[a, p, k].wait()
            origin = (at[three] - step) % 4
            piece = bufs[a].at[spans({one: ("half", k), two: None, three: origin}) + (pl.ds(r0, nr),)]
            copy = remote(
                piece, piece, s3_send.at[a, p, 2 + k], s3_recv.at[a, p, 2 + k], shifted(at, three, step)
            )
            copy.start()
            third_copies[a, p, 2 + k] = copy

    def gather_end(a):
        for p in range(3):
            for k in range(2):
                third_copies[a, p, 2 + k].wait()

    swap_end(2, 0, move_h)
    packed[0, 0, 0, 0, 0] = (pack(0) * norm_scale * gain[...].reshape(1, width)).astype(bf16)
    gather_first(0)
    swap_end(2, 1, move_c)
    packed[1, 0, 0, 0, 0] = (pack(1) * (grad_scale / 4.0)).astype(bf16)
    gather_first(1)
    gather_second(0)
    gather_second(1)
    for p in range(3):
        gather_third(0, p)
    for copy in weight_copies:
        copy.wait()
    core_copies = []
    for n, (buf, where) in enumerate(
        ((w_up, (slice(None), slice(None), own_units)), (w_dn, (slice(None), own_units)))
    ):
        copy = remote(buf.at[where], buf.at[where], core_send.at[n], core_recv.at[n], core)
        copy.start()
        core_copies.append(copy)
    for p in range(3):
        gather_pass_on(0, p)
        gather_third(1, p)
    for copy in core_copies:
        copy.wait()
    gather_end(0)

    tokens_here = 8 * CAP

    def streamed(buf, body):
        def fetch(j, slot):
            return pltpu.make_async_copy(buf.at[j // 2, j % 2], stream.at[slot], stream_sem.at[slot])

        fetch(0, 0).start()

        def turn(j, carry):
            slot = j % 2

            @pl.when(j < 7)
            def _():
                fetch(j + 1, 1 - slot).start()

            fetch(j, slot).wait()
            body(j, stream[slot].reshape(tokens_here, width))
            return carry

        lax.fori_loop(0, 8, turn, 0)

    acc[...] = jnp.zeros_like(acc)

    def forward(j, block):
        acc[...] += jnp.dot(block, w_up[j], preferred_element_type=f32)

    streamed(g_norm, forward)
    value = acc[...] / root_width
    sigma = 1.0 / (1.0 + jnp.exp(-value))
    slope[...] = sigma * (1.0 + value * (1.0 - sigma))
    hidden[...] = (value * sigma).astype(bf16)

    def down(j, carry):
        block = jnp.dot(hidden[...], w_dn[j], preferred_element_type=f32)
        part[j // 2, j % 2] = block.astype(bf16).reshape(4, 2, CAP, width)
        return carry

    lax.fori_loop(0, 8, down, 0)
    for p in range(3):
        gather_pass_on(1, p)

    sends = {}
    for p, (r0, nr) in enumerate(PARTS[2]):
        one, two, three = ORDERS[p]
        row = pl.ds(r0, nr)
        for k, step in enumerate((1, 3)):
            src = part.at[spans({one: (at[one] + 2) % 4, two: ("half", k), three: None}) + (row,)]
            sends[p, k] = remote(
                src, half_bufs[p].at[k], h_send.at[p, k], h_recv.at[p, k], shifted(at, one, step)
            )
            sends[p, k].start()
    for p, (r0, nr) in enumerate(PARTS[2]):
        one, two, three = ORDERS[p]
        row = pl.ds(r0, nr)
        for k, step in enumerate((1, 3)):
            other = 1 - k
            src = part.at[spans({one: (at[one] + step) % 4, two: ("half", other), three: None}) + (row,)]
            dst = full_bufs[p].at[(k,) + spans({one: 0, two: ("half", other), three: None})]
            sends[p, 2 + k] = remote(
                src, dst, f_send.at[p, k, 0], f_recv.at[p, k, 0], shifted(at, one, step)
            )
            sends[p, 2 + k].start()

    gather_end(1)
    acc[...] = jnp.zeros_like(acc)
    turned[...] = jnp.transpose(hidden[...])
    own_first = at["c"] == 0
    own_rows = pl.ds(pl.multiple_of(at["c"] * units, units), units)

    def give(buf, dst, send, recv, j):
        return remote(buf.at[j], dst.at[j], send.at[j], recv.at[j], core)

    def backward(j, block):
        acc[...] += lax.dot_general(block, w_dn[j], (((1,), (1,)), ((), ())), preferred_element_type=f32)
        grad = jnp.dot(turned[...], block, preferred_element_type=f32) * (step_size / root_units)
        low, high = grad[:units], grad[units:]
        own_dn[j] = w_dn[j, own_rows].astype(f32) - jnp.where(own_first, low, high)
        oth_dn[j] = jnp.where(own_first, high, low)
        give(oth_dn, got_dn, gd_send, gd_recv, j).start()

    streamed(g_out, backward)

    for p, (r0, nr) in enumerate(PARTS[2]):
        one, two, three = ORDERS[p]
        for k, step in enumerate((1, 3)):
            sends[p, k].wait()
            sel = {one: 0, two: ("half", k), three: None}
            dims = sizes(sel, nr, width)[:4]
            base = starts_of({one: (at[one] + step) % 4, two: ("half", k), three: None})

            def add(q, carry, p=p, k=k, dims=dims, base=base, r0=r0, nr=nr):
                ix = lead(q, dims)
                half_bufs[p][(k,) + ix] = (
                    half_bufs[p][(k,) + ix] + part[moved(base, ix) + (pl.ds(r0, nr),)]
                )
                return carry

            lax.fori_loop(0, count(dims), add, 0)
            dst = full_bufs[p].at[(k,) + spans(sel)]
            sends[p, 4 + k] = remote(
                half_bufs[p].at[k], dst, f_send.at[p, k, 1], f_recv.at[p, k, 1], shifted(at, one, step)
            )
            sends[p, 4 + k].start()

    turned[...] = jnp.transpose((acc[...] / root_units * slope[...]).astype(bf16))

    def up_grad(j, block):
        grad = jnp.dot(turned[...], block, preferred_element_type=f32) * (step_size / root_width)
        low, high = jnp.transpose(grad[:units]), jnp.transpose(grad[units:])
        weight = w_up[j].astype(f32)
        base = jnp.where(own_first, weight[:, :units], weight[:, units:])
        own_up[j] = base - jnp.where(own_first, low, high)
        oth_up[j] = jnp.where(own_first, high, low)
        give(oth_up, got_up, gu_send, gu_recv, j).start()

    streamed(g_norm, up_grad)

    def put_dn(j):
        return pltpu.make_async_copy(
            own_dn.at[j], new_dn.at[:, pl.ds(pl.multiple_of(j * width, 128), width)], nd_sem.at[j]
        )

    def put_up(j):
        return pltpu.make_async_copy(
            own_up.at[j], new_up.at[pl.ds(pl.multiple_of(j * width, 128), width)], nu_sem.at[j]
        )

    def finish_dn(j, carry):
        give(oth_dn, got_dn, gd_send, gd_recv, j).wait()
        own_dn[j] = own_dn[j] - got_dn[j]
        put_dn(j).start()
        return carry

    def finish_up(j, carry):
        give(oth_up, got_up, gu_send, gu_recv, j).wait()
        own_up[j] = own_up[j] - got_up[j]
        put_up(j).start()
        return carry

    lax.fori_loop(0, 8, finish_dn, 0)
    lax.fori_loop(0, 8, finish_up, 0)

    for p, (r0, nr) in enumerate(PARTS[2]):
        one, two, three = ORDERS[p]
        for n in (2, 3, 4, 5):
            sends[p, n].wait()
        for k, step in enumerate(OFFSETS + (0,)):
            spot = (at[two] + step) % 4
            dims = sizes({one: 0, two: 0, three: None}, nr, width)[:4]
            local = starts_of({one: 0, two: spot, three: None})
            base = starts_of({one: at[one], two: spot, three: None})

            def add(q, carry, p=p, dims=dims, local=local, base=base, r0=r0, nr=nr):
                ix = lead(q, dims)
                there = moved(local, ix)
                value = full_bufs[p][(0,) + there].astype(f32) + full_bufs[p][(1,) + there].astype(f32)
                value = value + part[moved(base, ix) + (pl.ds(r0, nr),)].astype(f32)
                full_bufs[p][(0,) + there] = value.astype(bf16)
                return carry

            lax.fori_loop(0, 4, add, 0)
            if step:
                src = full_bufs[p].at[(0,) + spans({one: 0, two: spot, three: None})]
                sends[p, 6 + k] = remote(
                    src, two_bufs[p].at[k], t_send.at[p, k], t_recv.at[p, k], shifted(at, two, step)
                )
                sends[p, 6 + k].start()
    for p, (r0, nr) in enumerate(PARTS[2]):
        one, two, three = ORDERS[p]
        for k in range(3):
            sends[p, 6 + k].wait()
        dims = sizes({one: 0, two: 0, three: None}, nr, width)[:4]
        local = starts_of({one: 0, two: at[two], three: None})
        for q in range(4):
            ix = lead(q, dims)
            value = full_bufs[p][(0,) + moved(local, ix)].astype(f32)
            for k in range(3):
                value = value + two_bufs[p][(k,) + ix].astype(f32)
            two_bufs[p][(0,) + ix] = value.astype(bf16)
        for k, step in enumerate(OFFSETS):
            src = two_bufs[p].at[(0,) + spans({one: 0, two: 0, three: (at[three] + step) % 4})]
            sends[p, 9 + k] = remote(
                src, one_bufs[p].at[k], o_send.at[p, k], o_recv.at[p, k], shifted(at, three, step)
            )
            sends[p, 9 + k].start()
    for p, (r0, nr) in enumerate(PARTS[2]):
        one, two, three = ORDERS[p]
        for k in range(3):
            sends[p, 9 + k].wait()
        there = starts_of({one: 0, two: 0, three: at[three]})
        value = two_bufs[p][(0,) + there].astype(f32)
        for k in range(3):
            value = value + one_bufs[p][k, 0, 0, 0, 0].astype(f32)
        tokens[pl.ds(r0, nr)] = (value / root_units).astype(bf16)
    for s in range(row_count):
        out[s] = lax.dot_general(
            masks[s], tokens[...], (((0,), (0,)), ((), ())), preferred_element_type=f32
        ).astype(bf16)

    def drain(j, carry):
        put_dn(j).wait()
        put_up(j).wait()
        return carry

    lax.fori_loop(0, 8, drain, 0)


def on_device(
    hidden_rows, cotangent, lengths, rewards, swap_rows, norm_gain, up_weight, down_weight
):
    row_count, slot_len, width = hidden_rows.shape
    root_width = math.sqrt(width * lax.axis_size("mp"))
    root_units = math.sqrt(up_weight.shape[1] * lax.axis_size("dp"))
    f32, bf16 = jnp.float32, jnp.bfloat16
    blocks = (4, 2, 4, 2, CAP, width)
    tokens = 8 * CAP
    dma = pltpu.SemaphoreType.DMA
    vmem = pl.BlockSpec(memory_space=pltpu.VMEM)
    smem = pl.BlockSpec(memory_space=pltpu.SMEM)
    hbm = pl.BlockSpec(memory_space=pl.ANY)
    half, full, two_b, one_b = [], [], [], []
    for (one, two, three), (_, nr) in zip(ORDERS, PARTS[2]):
        half.append(pltpu.VMEM((2,) + sizes({one: 0, two: ("half", 0), three: None}, nr, width), bf16))
        full.append(pltpu.VMEM((2,) + sizes({one: 0, two: None, three: None}, nr, width), bf16))
        two_b.append(pltpu.VMEM((3,) + sizes({one: 0, two: 0, three: None}, nr, width), bf16))
        one_b.append(pltpu.VMEM((3, 1, 1, 1, 1, nr, width), bf16))

    def body(*refs):
        step_kernel(root_width, root_units, *refs)

    block_out, new_up, new_dn, _, _ = pl.pallas_call(
        body,
        out_shape=(
            jax.ShapeDtypeStruct((row_count, slot_len, width), bf16),
            jax.ShapeDtypeStruct((8 * width, 128), f32),
            jax.ShapeDtypeStruct((128, 8 * width), f32),
            jax.ShapeDtypeStruct(blocks, bf16),
            jax.ShapeDtypeStruct(blocks, bf16),
        ),
        in_specs=[hbm, hbm, vmem, smem, smem, smem, hbm, hbm],
        out_specs=(vmem, hbm, hbm, hbm, hbm),
        scratch_shapes=[
            pltpu.VMEM((row_count, slot_len, width), bf16),
            pltpu.VMEM((row_count, slot_len, width), bf16),
            pltpu.VMEM((3, 2, 2, slot_len, width), bf16),
            pltpu.VMEM((3, 2, 2, slot_len, width), bf16),
            pltpu.VMEM((row_count, 8, 128), f32),
            pltpu.VMEM((3, 2, 8, 128), f32),
            pltpu.VMEM((3, 2, 8, 128), f32),
            pltpu.VMEM((8, 8, row_count * slot_len), f32),
            pltpu.VMEM((2, 1, 1, 1, 1, CAP, width), bf16),
            pltpu.VMEM((row_count, CAP, slot_len), bf16),
            pltpu.VMEM((8, width, 256), bf16),
            pltpu.VMEM((8, 256, width), bf16),
            pltpu.VMEM((2, 4, 2, CAP, width), bf16),
            pltpu.VMEM((tokens, 256), f32),
            pltpu.VMEM((tokens, 256), bf16),
            pltpu.VMEM((256, tokens), bf16),
            pltpu.VMEM((tokens, 256), f32),
            pltpu.VMEM(blocks, bf16),
            pltpu.VMEM((8, width, 128), f32),
            pltpu.VMEM((8, width, 128), f32),
            pltpu.VMEM((8, width, 128), f32),
            pltpu.VMEM((8, 128, width), f32),
            pltpu.VMEM((8, 128, width), f32),
            pltpu.VMEM((8, 128, width), f32),
            pltpu.VMEM((CAP, width), bf16),
        ] + half + full + two_b + one_b + [
            dma((7,)), dma((7,)), dma((3, 2)), dma((3, 2)), dma((3,)), dma((3,)),
            dma((7,)), dma((7,)), dma((7,)), dma((7,)), dma((6,)), dma((2,)), dma((2,)),
            dma((2, 3, 3)), dma((2, 3, 3)), dma((2, 3, 3)), dma((2, 3, 3)),
            dma((2, 3, 4)), dma((2, 3, 4)),
            dma((2,)), dma((8,)), dma((8,)), dma((8,)), dma((8,)), dma((8,)), dma((8,)),
            dma((3, 2)), dma((3, 2)), dma((3, 2, 2)), dma((3, 2, 2)),
            dma((3, 3)), dma((3, 3)), dma((3, 3)), dma((3, 3)),
        ],
        compiler_params=pltpu.CompilerParams(
            collective_id=1, has_side_effects=True, vmem_limit_bytes=60 << 20
        ),
        name="policy_step",
    )(
        hidden_rows, cotangent, norm_gain, lengths, rewards, swap_rows, up_weight, down_weight,
    )
    return (block_out, new_up, new_dn)


def solution(mesh):
    return jax.shard_map(
        on_device,
        mesh=mesh,
        in_specs=(
            P("dp", None, "mp"),
            P("dp", None, "mp"),
            P("dp"),
            P("dp"),
            P("dp", None, None),
            P("mp"),
            P("mp", "dp"),
            P("dp", "mp"),
        ),
        out_specs=(P("dp", None, "mp"), P(None, ("dp", "mp")), P(("dp", "mp"), None)),
        check_vma=False,
    )
```

```python
import math

import jax
import jax.numpy as jnp
from jax import lax
from jax.experimental import pallas as pl
from jax.experimental.pallas import tpu as pltpu
from jax.sharding import PartitionSpec as P

norm_eps = 1e-06
step_size = 4.0
MESH = pl.DeviceIdType.MESH

CAP = 128
ORDERS = (("x", "y", "z"), ("y", "z", "x"), ("z", "x", "y"))


def cut_block(last, *columns):
    chunks = []
    for c0, nc, rows in columns:
        r0 = 0
        for axis, nr in zip("xyz", rows):
            chunks.append((last[axis], r0, nr, c0, nc))
            r0 += nr
    return tuple(chunks)


GATHER_LAST = {"z": 0, "x": 1, "y": 2}
SCATTER_FIRST = {"x": 0, "y": 1, "z": 2}
PARTS = (
    cut_block(GATHER_LAST, (0, 640, (48, 48, 32))),
    cut_block(GATHER_LAST, (0, 640, (48, 32, 48))),
    cut_block(SCATTER_FIRST, (0, 384, (32, 48, 48)), (384, 256, (64, 32, 32))),
)
CHUNKS = len(PARTS[2])
MOST = max(len(chunks) for chunks in PARTS)
OFFSETS = (1, 3, 2)


def place():
    i = lax.axis_index("dp")
    j = lax.axis_index("mp")
    return {
        "x": i // 4,
        "y": j // 2,
        "z": ((i // 2) % 2) * 2 + j % 2,
        "c": i % 2,
    }


def device(at):
    z = at["z"]
    return ((at["x"] * 2 + z // 2) * 2 + at["c"], at["y"] * 2 + z % 2)


def shifted(at, axis, step):
    count = 2 if axis == "c" else 4
    return {**at, axis: (at[axis] + step) % count}


def spans(sel):
    def plain(s):
        if isinstance(s, tuple):
            return pl.ds(2 * s[1], 2)
        return pl.ds(0, 4) if s is None else pl.ds(s, 1)

    z = sel["z"]
    if z is None:
        z_lo, z_hi = pl.ds(0, 2), pl.ds(0, 2)
    elif isinstance(z, tuple):
        z_lo, z_hi = pl.ds(0, 2), pl.ds(z[1], 1)
    else:
        z_lo, z_hi = pl.ds(z % 2, 1), pl.ds(z // 2, 1)
    return (plain(sel["y"]), z_lo, plain(sel["x"]), z_hi)


def remote(src, dst, send, recv, at):
    return pltpu.make_async_remote_copy(
        src_ref=src,
        dst_ref=dst,
        send_sem=send,
        recv_sem=recv,
        device_id=device(at),
        device_id_type=MESH,
    )


def knock(peers):
    barrier = pltpu.get_barrier_semaphore()
    for at in peers:
        pl.semaphore_signal(barrier, inc=1, device_id=device(at), device_id_type=MESH)


def enter(peers):
    pl.semaphore_wait(pltpu.get_barrier_semaphore(), len(peers))


def axis_peers(at):
    return [shifted(at, axis, k) for axis in "xyz" for k in OFFSETS]


def row_mask(meta, slot, slot_len):
    length = meta[slot, 0:1, 0:1]
    start = jnp.zeros((1, 1), jnp.float32)
    for before in range(slot):
        start = start + meta[before, 0:1, 0:1]
    token = lax.broadcasted_iota(jnp.int32, (CAP, slot_len), 0).astype(jnp.float32)
    spot = lax.broadcasted_iota(jnp.int32, (CAP, slot_len), 1).astype(jnp.float32)
    return jnp.logical_and(token == spot + start, spot < length)


def sizes(sel, nr, width):
    def plain(s):
        return 2 if isinstance(s, tuple) else (4 if s is None else 1)

    z = sel["z"]
    z_dims = (2, 2) if z is None else ((2, 1) if isinstance(z, tuple) else (1, 1))
    return (plain(sel["y"]), z_dims[0], plain(sel["x"]), z_dims[1], nr, width)


def lead(q, dims):
    d = q % dims[3]
    q = q // dims[3]
    c = q % dims[2]
    q = q // dims[2]
    b = q % dims[1]
    return (q // dims[1], b, c, d)


def starts_of(sel):
    return tuple(s.start for s in spans(sel))


def moved(base, ix):
    return tuple(s + i for s, i in zip(base, ix))


def count(dims):
    return dims[0] * dims[1] * dims[2] * dims[3]


def unit_slope(preact):
    sigma = 1.0 / (1.0 + jnp.exp(-preact))
    return sigma * (1.0 + preact * (1.0 - sigma))


def step_kernel(
    root_width, root_units,
    hid, cot, gain_in, lens_in, rew_in, swp_in, up, dn,
    out, new_up, new_dn, g_norm, g_out,
    h_rows, c_rows, out_rows, in_rows, meta, out_meta, in_meta, squares, packed, masks,
    w_up, w_dn, stream, acc, hidden, turned, slope, part,
    own_up, oth_up, got_up, own_dn, oth_dn, got_dn, tokens,
    relay_up, relay_dn, gain, lens, rew, swp, *more
):
    half_bufs, full_bufs, two_bufs, one_bufs = (more[CHUNKS * n : CHUNKS * (n + 1)] for n in range(4))
    (
        sq_send, sq_recv, swap_send, swap_recv, meta_send, meta_recv,
        wy_send, wy_recv, wz_send, wz_recv, local_sem, core_send, core_recv,
        s1_send, s1_recv, s2_send, s2_recv, s3_send, s3_recv,
        stream_sem, gu_send, gu_recv, gd_send, gd_recv, nu_sem, nd_sem,
        h_send, h_recv, f_send, f_recv, t_send, t_recv, o_send, o_recv,
    ) = more[4 * CHUNKS :]
    at = place()
    row_count, slot_len, width = hid.shape
    units = 128
    f32, bf16 = jnp.float32, jnp.bfloat16

    loads = [
        pltpu.make_async_copy(src, dst, local_sem.at[4 + n])
        for n, (src, dst) in enumerate((
            (swp_in, swp), (hid, h_rows), (cot, c_rows), (lens_in, lens), (rew_in, rew), (gain_in, gain)
        ))
    ]
    for copy in loads:
        copy.start()
    mp_peers = [
        {**shifted(at, "y", dy), "z": (at["z"] // 2) * 2 + (at["z"] % 2 + dz) % 2}
        for dy in range(4) for dz in range(2) if dy or dz
    ]
    diagonal = [p for n, p in enumerate(mp_peers) if n in (2, 4, 6)]
    core = shifted(at, "c", 1)
    peers = axis_peers(at) + diagonal + [core]
    knock(peers)
    partners = (core, shifted(at, "z", 2), {**at, "x": (at["x"] // 2) * 2 + 1 - at["x"] % 2})

    store = (h_rows, c_rows)

    def swap_pick(r, a):
        out_rows[r, a, 0] = store[a][swp[0, r, 0]]
        out_rows[r, a, 1] = store[a][swp[0, r, 1]]

    def swap_start(r, a):
        if r:
            swap_pick(r, a)
        copy = remote(
            out_rows.at[r, a], in_rows.at[r, a], swap_send.at[r, a], swap_recv.at[r, a], partners[r]
        )
        copy.start()
        return copy

    def swap_end(r, a, copy):
        copy.wait()
        first, second = swp[0, r, 0], swp[0, r, 1]
        for s in range(row_count):
            store[a][s] = jnp.where(
                first == s, in_rows[r, a, 0], jnp.where(second == s, in_rows[r, a, 1], store[a][s])
            )

    def meta_start(r):
        out_meta[r, 0] = meta[swp[0, r, 0]]
        out_meta[r, 1] = meta[swp[0, r, 1]]
        copy = remote(out_meta.at[r], in_meta.at[r], meta_send.at[r], meta_recv.at[r], partners[r])
        copy.start()
        return copy

    def meta_end(r, copy):
        copy.wait()
        first, second = swp[0, r, 0], swp[0, r, 1]
        for s in range(row_count):
            meta[s] = jnp.where(first == s, in_meta[r, 0], jnp.where(second == s, in_meta[r, 1], meta[s]))

    def units_of(y, z_lo):
        return pl.ds(pl.multiple_of((y * 2 + z_lo) * units, units), units)

    z_lo = at["z"] % 2
    beside = {**at, "z": at["z"] + 1 - 2 * z_lo}
    own_units = pl.ds(pl.multiple_of(at["c"] * units, units), units)

    def weights_along_y():
        copies = {}
        for dy in (1, 3, 2):
            peer = shifted(at, "y", dy)
            near, far = units_of(peer["y"], z_lo), units_of(peer["y"], 1 - z_lo)
            moves = (
                (up.at[:, near], w_up.at[at["y"], z_lo, :, own_units]),
                (dn.at[near], w_dn.at[at["y"], z_lo, own_units]),
                (up.at[:, far], relay_up.at[at["y"]]),
                (dn.at[far], relay_dn.at[at["y"]]),
            )
            for n, (src, dst) in enumerate(moves):
                copy = remote(src, dst, wy_send.at[dy - 1, n], wy_recv.at[dy - 1, n], peer)
                copy.start()
                copies[dy, n] = copy
        near = units_of(at["y"], z_lo)
        for n, (src, dst) in enumerate(
            ((up.at[:, near], w_up.at[at["y"], z_lo, :, own_units]), (dn.at[near], w_dn.at[at["y"], z_lo, own_units]))
        ):
            copies[0, n] = pltpu.make_async_copy(src, dst, local_sem.at[n])
            copies[0, n].start()
        return copies

    def weights_along_z(dy):
        y = (at["y"] - dy) % 4
        far = units_of(y, 1 - z_lo)
        from_up = relay_up.at[y] if dy else up.at[:, far]
        from_dn = relay_dn.at[y] if dy else dn.at[far]
        copies = [
            remote(from_up, w_up.at[y, z_lo, :, own_units], wz_send.at[dy, 0], wz_recv.at[dy, 0], beside),
            remote(from_dn, w_dn.at[y, z_lo, own_units], wz_send.at[dy, 1], wz_recv.at[dy, 1], beside),
        ]
        for copy in copies:
            copy.start()
        return copies

    def weights_to_core(n, which):
        copies = [
            remote(
                w_up.at[:, which, :, own_units], w_up.at[:, which, :, own_units],
                core_send.at[n, 0], core_recv.at[n, 0], core,
            ),
            remote(
                w_dn.at[:, which, own_units], w_dn.at[:, which, own_units],
                core_send.at[n, 1], core_recv.at[n, 1], core,
            ),
        ]
        for copy in copies:
            copy.start()
        return copies

    for copy in loads:
        copy.wait()
    swap_pick(0, 0)
    swap_pick(0, 1)
    flat = h_rows[...].reshape(row_count * slot_len, width).astype(f32)
    squares[7] = lax.dot_general(
        jnp.ones((8, width), f32), flat * flat, (((1,), (1,)), ((), ())),
        precision=lax.Precision.HIGHEST, preferred_element_type=f32,
    )
    enter(peers)
    move_h = swap_start(0, 0)
    sq_copies = []
    for n, peer in enumerate(mp_peers):
        copy = remote(squares.at[7], squares.at[n], sq_send.at[n], sq_recv.at[n], peer)
        copy.start()
        sq_copies.append(copy)
    move_c = swap_start(0, 1)
    y_copies = weights_along_y()
    swap_end(0, 0, move_h)
    move_h = swap_start(1, 0)
    total = squares[7]
    for n, copy in enumerate(sq_copies):
        copy.wait()
        total = total + squares[n]
    factor = lax.rsqrt(total / (8 * width) + norm_eps)
    for s in range(row_count):
        meta[s, 0:1] = jnp.full((1, 128), lens[s].astype(f32), f32)
        meta[s, 1:2] = jnp.full((1, 128), rew[s].astype(f32), f32)
        meta[s, 2:8] = jnp.zeros((6, 128), f32)
        meta[s, 2:3, 0:slot_len] = factor[0:1, s * slot_len : (s + 1) * slot_len]
    move_m = meta_start(0)
    swap_end(0, 1, move_c)
    move_c = swap_start(1, 1)
    meta_end(0, move_m)
    move_m = meta_start(1)
    z_copies = weights_along_z(0)

    swap_end(1, 0, move_h)
    move_h = swap_start(2, 0)
    swap_end(1, 1, move_c)
    move_c = swap_start(2, 1)
    for dy in (1, 3):
        for n in (2, 3):
            y_copies[dy, n].wait()
        z_copies += weights_along_z(dy)
    meta_end(1, move_m)
    move_m = meta_start(2)
    meta_end(2, move_m)
    norm_scale = jnp.zeros((CAP, 1), f32)
    grad_scale = jnp.zeros((CAP, 1), f32)
    for s in range(row_count):
        hit = row_mask(meta, s, slot_len)
        masks[s] = jnp.where(hit, 1.0, 0.0).astype(bf16)
        norm_scale += jnp.sum(jnp.where(hit, meta[s, 2:3, 0:slot_len], 0.0), axis=1, keepdims=True)
        grad_scale += jnp.sum(jnp.where(hit, meta[s, 1:2, 0:slot_len], 0.0), axis=1, keepdims=True)

    def pack(a):
        picked = jnp.zeros((CAP, width), f32)
        for s in range(row_count):
            picked = picked + jnp.dot(masks[s], store[a][s], preferred_element_type=f32)
        return picked

    here = spans({k: at[k] for k in "xyz"})
    bufs = (g_norm, g_out)
    own, first_copies, second_copies, third_copies = [], {}, {}, {}

    def gather_first(a):
        copy = pltpu.make_async_copy(packed.at[a], bufs[a].at[here], local_sem.at[2 + a])
        copy.start()
        own.append(copy)
        for n, (p, r0, nr, c0, nc) in enumerate(PARTS[a]):
            for k, step in enumerate(OFFSETS):
                spot = (pl.ds(r0, nr), pl.ds(c0, nc))
                copy = remote(
                    packed.at[(a,) + (slice(None),) * 4 + spot], bufs[a].at[here + spot],
                    s1_send.at[a, n, k], s1_recv.at[a, n, k], shifted(at, ORDERS[p][0], step),
                )
                copy.start()
                first_copies[a, n, k] = copy

    def gather_second(a):
        own[a].wait()
        for n, (p, r0, nr, c0, nc) in enumerate(PARTS[a]):
            for k in range(3):
                first_copies[a, n, k].wait()
            one, two, three = ORDERS[p]
            spot = (pl.ds(r0, nr), pl.ds(c0, nc))
            piece = bufs[a].at[spans({one: None, two: at[two], three: at[three]}) + spot]
            for k, step in enumerate(OFFSETS):
                copy = remote(
                    piece, piece, s2_send.at[a, n, k], s2_recv.at[a, n, k], shifted(at, two, step)
                )
                copy.start()
                second_copies[a, n, k] = copy

    def gather_third(a, n):
        p, r0, nr, c0, nc = PARTS[a][n]
        for k in range(3):
            second_copies[a, n, k].wait()
        one, two, three = ORDERS[p]
        spot = (pl.ds(r0, nr), pl.ds(c0, nc))
        piece = bufs[a].at[spans({one: None, two: None, three: at[three]}) + spot]
        for k, step in enumerate((1, 3)):
            copy = remote(
                piece, piece, s3_send.at[a, n, k], s3_recv.at[a, n, k], shifted(at, three, step)
            )
            copy.start()
            third_copies[a, n, k] = copy

    def gather_pass_on(a, n):
        p, r0, nr, c0, nc = PARTS[a][n]
        one, two, three = ORDERS[p]
        spot = (pl.ds(r0, nr), pl.ds(c0, nc))
        for k, step in enumerate((1, 3)):
            third_copies[a, n, k].wait()
            origin = (at[three] - step) % 4
            piece = bufs[a].at[spans({one: ("half", k), two: None, three: origin}) + spot]
            copy = remote(
                piece, piece, s3_send.at[a, n, 2 + k], s3_recv.at[a, n, 2 + k], shifted(at, three, step)
            )
            copy.start()
            third_copies[a, n, 2 + k] = copy

    def gather_end(a):
        for n in range(len(PARTS[a])):
            for k in range(2):
                third_copies[a, n, 2 + k].wait()

    swap_end(2, 0, move_h)
    packed[0, 0, 0, 0, 0] = (pack(0) * norm_scale * gain[...].reshape(1, width)).astype(bf16)
    gather_first(0)
    swap_end(2, 1, move_c)
    packed[1, 0, 0, 0, 0] = (pack(1) * (grad_scale / 4.0)).astype(bf16)
    gather_first(1)
    gather_second(0)
    for n in (2, 3):
        y_copies[2, n].wait()
    z_copies += weights_along_z(2)
    gather_second(1)
    for n in range(len(PARTS[0])):
        gather_third(0, n)
    for dy in range(4):
        for n in range(2):
            y_copies[dy, n].wait()
    core_copies = weights_to_core(0, z_lo)
    for n in range(len(PARTS[0])):
        gather_pass_on(0, n)
    for n in range(len(PARTS[1])):
        gather_third(1, n)
    for copy in z_copies:
        copy.wait()
    core_copies += weights_to_core(1, 1 - z_lo)
    gather_end(0)
    for copy in core_copies:
        copy.wait()

    tokens_here = 8 * CAP

    def streamed(buf, body):
        def fetch(j, slot):
            return pltpu.make_async_copy(buf.at[j // 2, j % 2], stream.at[slot], stream_sem.at[slot])

        fetch(0, 0).start()

        def turn(j, carry):
            slot = j % 2

            @pl.when(j < 7)
            def _():
                fetch(j + 1, 1 - slot).start()

            fetch(j, slot).wait()
            body(j, stream[slot].reshape(tokens_here, width))
            return carry

        lax.fori_loop(0, 8, turn, 0)

    acc[...] = jnp.zeros_like(acc)

    def forward(j, block):
        acc[...] += jnp.dot(block, w_up[j // 2, j % 2], preferred_element_type=f32)

    streamed(g_norm, forward)
    value = acc[...] / root_width
    sigma = 1.0 / (1.0 + jnp.exp(-value))
    slope[...] = sigma * (1.0 + value * (1.0 - sigma))
    hidden[...] = (value * sigma).astype(bf16)

    def down(j, carry):
        block = jnp.dot(hidden[...], w_dn[j // 2, j % 2], preferred_element_type=f32)
        part[j // 2, j % 2] = block.astype(bf16).reshape(4, 2, CAP, width)
        return carry

    lax.fori_loop(0, 8, down, 0)
    for n in range(len(PARTS[1])):
        gather_pass_on(1, n)

    sends = {}
    for n, (p, r0, nr, c0, nc) in enumerate(PARTS[2]):
        one, two, three = ORDERS[p]
        spot = (pl.ds(r0, nr), pl.ds(c0, nc))
        for k, step in enumerate((1, 3)):
            src = part.at[spans({one: (at[one] + 2) % 4, two: ("half", k), three: None}) + spot]
            sends[n, k] = remote(
                src, half_bufs[n].at[k], h_send.at[n, k], h_recv.at[n, k], shifted(at, one, step)
            )
            sends[n, k].start()
    for n, (p, r0, nr, c0, nc) in enumerate(PARTS[2]):
        one, two, three = ORDERS[p]
        spot = (pl.ds(r0, nr), pl.ds(c0, nc))
        for k, step in enumerate((1, 3)):
            other = 1 - k
            src = part.at[spans({one: (at[one] + step) % 4, two: ("half", other), three: None}) + spot]
            dst = full_bufs[n].at[(k,) + spans({one: 0, two: ("half", other), three: None})]
            sends[n, 2 + k] = remote(
                src, dst, f_send.at[n, k, 0], f_recv.at[n, k, 0], shifted(at, one, step)
            )
            sends[n, 2 + k].start()

    gather_end(1)
    acc[...] = jnp.zeros_like(acc)
    turned[...] = jnp.transpose(hidden[...])
    own_first = at["c"] == 0
    own_rows = pl.ds(pl.multiple_of(at["c"] * units, units), units)

    def give(buf, dst, send, recv, j):
        return remote(buf.at[j], dst.at[j], send.at[j], recv.at[j], core)

    def backward(j, block):
        acc[...] += lax.dot_general(block, w_dn[j // 2, j % 2], (((1,), (1,)), ((), ())), preferred_element_type=f32)
        grad = jnp.dot(turned[...], block, preferred_element_type=f32) * (step_size / root_units)
        low, high = grad[:units], grad[units:]
        own_dn[j] = w_dn[j // 2, j % 2, own_rows].astype(f32) - jnp.where(own_first, low, high)
        oth_dn[j] = jnp.where(own_first, high, low)
        give(oth_dn, got_dn, gd_send, gd_recv, j).start()

    streamed(g_out, backward)

    for n, (p, r0, nr, c0, nc) in enumerate(PARTS[2]):
        one, two, three = ORDERS[p]
        spot = (pl.ds(r0, nr), pl.ds(c0, nc))
        for k, step in enumerate((1, 3)):
            sends[n, k].wait()
            sel = {one: 0, two: ("half", k), three: None}
            dims = sizes(sel, nr, nc)[:4]
            base = starts_of({one: (at[one] + step) % 4, two: ("half", k), three: None})

            def add(q, carry, n=n, k=k, dims=dims, base=base, spot=spot):
                ix = lead(q, dims)
                half_bufs[n][(k,) + ix] = half_bufs[n][(k,) + ix] + part[moved(base, ix) + spot]
                return carry

            lax.fori_loop(0, count(dims), add, 0)
            dst = full_bufs[n].at[(k,) + spans(sel)]
            sends[n, 4 + k] = remote(
                half_bufs[n].at[k], dst, f_send.at[n, k, 1], f_recv.at[n, k, 1], shifted(at, one, step)
            )
            sends[n, 4 + k].start()

    turned[...] = jnp.transpose((acc[...] / root_units * slope[...]).astype(bf16))

    def up_grad(j, block):
        grad = jnp.dot(turned[...], block, preferred_element_type=f32) * (step_size / root_width)
        low, high = jnp.transpose(grad[:units]), jnp.transpose(grad[units:])
        weight = w_up[j // 2, j % 2].astype(f32)
        base = jnp.where(own_first, weight[:, :units], weight[:, units:])
        own_up[j] = base - jnp.where(own_first, low, high)
        oth_up[j] = jnp.where(own_first, high, low)
        give(oth_up, got_up, gu_send, gu_recv, j).start()

    streamed(g_norm, up_grad)

    def put_dn(j):
        return pltpu.make_async_copy(
            own_dn.at[j], new_dn.at[:, pl.ds(pl.multiple_of(j * width, 128), width)], nd_sem.at[j]
        )

    def put_up(j):
        return pltpu.make_async_copy(
            own_up.at[j], new_up.at[pl.ds(pl.multiple_of(j * width, 128), width)], nu_sem.at[j]
        )

    def finish_dn(j, carry):
        give(oth_dn, got_dn, gd_send, gd_recv, j).wait()
        own_dn[j] = own_dn[j] - got_dn[j]
        put_dn(j).start()
        return carry

    def finish_up(j, carry):
        give(oth_up, got_up, gu_send, gu_recv, j).wait()
        own_up[j] = own_up[j] - got_up[j]
        put_up(j).start()
        return carry

    lax.fori_loop(0, 8, finish_dn, 0)
    lax.fori_loop(0, 8, finish_up, 0)

    for n, (p, r0, nr, c0, nc) in enumerate(PARTS[2]):
        one, two, three = ORDERS[p]
        spot = (pl.ds(r0, nr), pl.ds(c0, nc))
        for m in (2, 3, 4, 5):
            sends[n, m].wait()
        for k, step in enumerate(OFFSETS + (0,)):
            index = (at[two] + step) % 4
            dims = sizes({one: 0, two: 0, three: None}, nr, nc)[:4]
            local = starts_of({one: 0, two: index, three: None})
            base = starts_of({one: at[one], two: index, three: None})

            def add(q, carry, n=n, dims=dims, local=local, base=base, spot=spot):
                ix = lead(q, dims)
                there = moved(local, ix)
                value = full_bufs[n][(0,) + there].astype(f32) + full_bufs[n][(1,) + there].astype(f32)
                value = value + part[moved(base, ix) + spot].astype(f32)
                full_bufs[n][(0,) + there] = value.astype(bf16)
                return carry

            lax.fori_loop(0, 4, add, 0)
            if step:
                src = full_bufs[n].at[(0,) + spans({one: 0, two: index, three: None})]
                sends[n, 6 + k] = remote(
                    src, two_bufs[n].at[k], t_send.at[n, k], t_recv.at[n, k], shifted(at, two, step)
                )
                sends[n, 6 + k].start()
    for n, (p, r0, nr, c0, nc) in enumerate(PARTS[2]):
        one, two, three = ORDERS[p]
        for k in range(3):
            sends[n, 6 + k].wait()
        dims = sizes({one: 0, two: 0, three: None}, nr, nc)[:4]
        local = starts_of({one: 0, two: at[two], three: None})
        for q in range(4):
            ix = lead(q, dims)
            value = full_bufs[n][(0,) + moved(local, ix)].astype(f32)
            for k in range(3):
                value = value + two_bufs[n][(k,) + ix].astype(f32)
            two_bufs[n][(0,) + ix] = value.astype(bf16)
        for k, step in enumerate(OFFSETS):
            src = two_bufs[n].at[(0,) + spans({one: 0, two: 0, three: (at[three] + step) % 4})]
            sends[n, 9 + k] = remote(
                src, one_bufs[n].at[k], o_send.at[n, k], o_recv.at[n, k], shifted(at, three, step)
            )
            sends[n, 9 + k].start()
    for n, (p, r0, nr, c0, nc) in enumerate(PARTS[2]):
        one, two, three = ORDERS[p]
        for k in range(3):
            sends[n, 9 + k].wait()
        there = starts_of({one: 0, two: 0, three: at[three]})
        value = two_bufs[n][(0,) + there].astype(f32)
        for k in range(3):
            value = value + one_bufs[n][k, 0, 0, 0, 0].astype(f32)
        tokens[pl.ds(r0, nr), pl.ds(c0, nc)] = (value / root_units).astype(bf16)
    for s in range(row_count):
        out[s] = lax.dot_general(
            masks[s], tokens[...], (((0,), (0,)), ((), ())), preferred_element_type=f32
        ).astype(bf16)

    def drain(j, carry):
        put_dn(j).wait()
        put_up(j).wait()
        return carry

    lax.fori_loop(0, 8, drain, 0)


def on_device(
    hidden_rows, cotangent, lengths, rewards, swap_rows, norm_gain, up_weight, down_weight
):
    row_count, slot_len, width = hidden_rows.shape
    root_width = math.sqrt(width * lax.axis_size("mp"))
    root_units = math.sqrt(up_weight.shape[1] * lax.axis_size("dp"))
    f32, bf16 = jnp.float32, jnp.bfloat16
    blocks = (4, 2, 4, 2, CAP, width)
    tokens = 8 * CAP
    dma = pltpu.SemaphoreType.DMA
    vmem = pl.BlockSpec(memory_space=pltpu.VMEM)
    hbm = pl.BlockSpec(memory_space=pl.ANY)
    half, full, two_b, one_b = [], [], [], []
    for p, _, nr, _, nc in PARTS[2]:
        one, two, three = ORDERS[p]
        half.append(pltpu.VMEM((2,) + sizes({one: 0, two: ("half", 0), three: None}, nr, nc), bf16))
        full.append(pltpu.VMEM((2,) + sizes({one: 0, two: None, three: None}, nr, nc), bf16))
        two_b.append(pltpu.VMEM((3,) + sizes({one: 0, two: 0, three: None}, nr, nc), bf16))
        one_b.append(pltpu.VMEM((3, 1, 1, 1, 1, nr, nc), bf16))

    def body(*refs):
        step_kernel(root_width, root_units, *refs)

    block_out, new_up, new_dn, _, _ = pl.pallas_call(
        body,
        out_shape=(
            jax.ShapeDtypeStruct((row_count, slot_len, width), bf16),
            jax.ShapeDtypeStruct((8 * width, 128), f32),
            jax.ShapeDtypeStruct((128, 8 * width), f32),
            jax.ShapeDtypeStruct(blocks, bf16),
            jax.ShapeDtypeStruct(blocks, bf16),
        ),
        in_specs=[hbm] * 8,
        out_specs=(vmem, hbm, hbm, hbm, hbm),
        scratch_shapes=[
            pltpu.VMEM((row_count, slot_len, width), bf16),
            pltpu.VMEM((row_count, slot_len, width), bf16),
            pltpu.VMEM((3, 2, 2, slot_len, width), bf16),
            pltpu.VMEM((3, 2, 2, slot_len, width), bf16),
            pltpu.VMEM((row_count, 8, 128), f32),
            pltpu.VMEM((3, 2, 8, 128), f32),
            pltpu.VMEM((3, 2, 8, 128), f32),
            pltpu.VMEM((8, 8, row_count * slot_len), f32),
            pltpu.VMEM((2, 1, 1, 1, 1, CAP, width), bf16),
            pltpu.VMEM((row_count, CAP, slot_len), bf16),
            pltpu.VMEM((4, 2, width, 256), bf16),
            pltpu.VMEM((4, 2, 256, width), bf16),
            pltpu.VMEM((2, 4, 2, CAP, width), bf16),
            pltpu.VMEM((tokens, 256), f32),
            pltpu.VMEM((tokens, 256), bf16),
            pltpu.VMEM((256, tokens), bf16),
            pltpu.VMEM((tokens, 256), f32),
            pltpu.VMEM(blocks, bf16),
            pltpu.VMEM((8, width, 128), f32),
            pltpu.VMEM((8, width, 128), f32),
            pltpu.VMEM((8, width, 128), f32),
            pltpu.VMEM((8, 128, width), f32),
            pltpu.VMEM((8, 128, width), f32),
            pltpu.VMEM((8, 128, width), f32),
            pltpu.VMEM((CAP, width), bf16),
            pltpu.VMEM((4, width, 128), bf16),
            pltpu.VMEM((4, 128, width), bf16),
            pltpu.VMEM((width,), f32),
            pltpu.SMEM((row_count,), jnp.int32),
            pltpu.SMEM((row_count,), jnp.int32),
            pltpu.SMEM((1, 3, 2), jnp.int32),
        ] + half + full + two_b + one_b + [
            dma((7,)), dma((7,)), dma((3, 2)), dma((3, 2)), dma((3,)), dma((3,)),
            dma((3, 4)), dma((3, 4)), dma((4, 2)), dma((4, 2)), dma((10,)), dma((2, 2)), dma((2, 2)),
            dma((2, MOST, 3)), dma((2, MOST, 3)), dma((2, MOST, 3)), dma((2, MOST, 3)),
            dma((2, MOST, 4)), dma((2, MOST, 4)),
            dma((2,)), dma((8,)), dma((8,)), dma((8,)), dma((8,)), dma((8,)), dma((8,)),
            dma((CHUNKS, 2)), dma((CHUNKS, 2)), dma((CHUNKS, 2, 2)), dma((CHUNKS, 2, 2)),
            dma((CHUNKS, 3)), dma((CHUNKS, 3)), dma((CHUNKS, 3)), dma((CHUNKS, 3)),
        ],
        compiler_params=pltpu.CompilerParams(
            collective_id=1, has_side_effects=True, vmem_limit_bytes=60 << 20
        ),
        name="policy_step",
    )(
        hidden_rows, cotangent, norm_gain, lengths, rewards, swap_rows, up_weight, down_weight,
    )
    return (block_out, new_up, new_dn)


def solution(mesh):
    return jax.shard_map(
        on_device,
        mesh=mesh,
        in_specs=(
            P("dp", None, "mp"),
            P("dp", None, "mp"),
            P("dp"),
            P("dp"),
            P("dp", None, None),
            P("mp"),
            P("mp", "dp"),
            P("dp", "mp"),
        ),
        out_specs=(P("dp", None, "mp"), P(None, ("dp", "mp")), P(("dp", "mp"), None)),
        check_vma=False,
    )
```

```python
import math

import jax
import jax.numpy as jnp
from jax import lax
from jax.experimental import pallas as pl
from jax.experimental.pallas import tpu as pltpu
from jax.sharding import PartitionSpec as P

norm_eps = 1e-06
step_size = 4.0
MESH = pl.DeviceIdType.MESH

CAP = 128
ORDERS = (("x", "y", "z"), ("y", "z", "x"), ("z", "x", "y"))


def cut_block(last, *columns):
    chunks = []
    for c0, nc, rows in columns:
        r0 = 0
        for axis, nr in zip("xyz", rows):
            chunks.append((last[axis], r0, nr, c0, nc))
            r0 += nr
    return tuple(chunks)


GATHER_LAST = {"z": 0, "x": 1, "y": 2}
SCATTER_FIRST = {"x": 0, "y": 1, "z": 2}
PARTS = (
    cut_block(GATHER_LAST, (0, 640, (48, 48, 32))),
    cut_block(GATHER_LAST, (0, 384, (48, 32, 48)), (384, 256, (32, 48, 48))),
    cut_block(SCATTER_FIRST, (0, 384, (32, 48, 48)), (384, 256, (64, 32, 32))),
)
CHUNKS = len(PARTS[2])
MOST = max(len(chunks) for chunks in PARTS)
OFFSETS = (1, 3, 2)


def place():
    i = lax.axis_index("dp")
    j = lax.axis_index("mp")
    return {
        "x": i // 4,
        "y": j // 2,
        "z": ((i // 2) % 2) * 2 + j % 2,
        "c": i % 2,
    }


def device(at):
    z = at["z"]
    return ((at["x"] * 2 + z // 2) * 2 + at["c"], at["y"] * 2 + z % 2)


def shifted(at, axis, step):
    count = 2 if axis == "c" else 4
    return {**at, axis: (at[axis] + step) % count}


def spans(sel):
    def plain(s):
        if isinstance(s, tuple):
            return pl.ds(2 * s[1], 2)
        return pl.ds(0, 4) if s is None else pl.ds(s, 1)

    z = sel["z"]
    if z is None:
        z_lo, z_hi = pl.ds(0, 2), pl.ds(0, 2)
    elif isinstance(z, tuple):
        z_lo, z_hi = pl.ds(0, 2), pl.ds(z[1], 1)
    else:
        z_lo, z_hi = pl.ds(z % 2, 1), pl.ds(z // 2, 1)
    return (plain(sel["y"]), z_lo, plain(sel["x"]), z_hi)


def remote(src, dst, send, recv, at):
    return pltpu.make_async_remote_copy(
        src_ref=src,
        dst_ref=dst,
        send_sem=send,
        recv_sem=recv,
        device_id=device(at),
        device_id_type=MESH,
    )


def knock(peers):
    barrier = pltpu.get_barrier_semaphore()
    for at in peers:
        pl.semaphore_signal(barrier, inc=1, device_id=device(at), device_id_type=MESH)


def enter(peers):
    pl.semaphore_wait(pltpu.get_barrier_semaphore(), len(peers))


def axis_peers(at):
    return [shifted(at, axis, k) for axis in "xyz" for k in OFFSETS]


def row_mask(meta, slot, slot_len):
    length = meta[slot, 0:1, 0:1]
    start = jnp.zeros((1, 1), jnp.float32)
    for before in range(slot):
        start = start + meta[before, 0:1, 0:1]
    token = lax.broadcasted_iota(jnp.int32, (CAP, slot_len), 0).astype(jnp.float32)
    spot = lax.broadcasted_iota(jnp.int32, (CAP, slot_len), 1).astype(jnp.float32)
    return jnp.logical_and(token == spot + start, spot < length)


def sizes(sel, nr, width):
    def plain(s):
        return 2 if isinstance(s, tuple) else (4 if s is None else 1)

    z = sel["z"]
    z_dims = (2, 2) if z is None else ((2, 1) if isinstance(z, tuple) else (1, 1))
    return (plain(sel["y"]), z_dims[0], plain(sel["x"]), z_dims[1], nr, width)


def lead(q, dims):
    d = q % dims[3]
    q = q // dims[3]
    c = q % dims[2]
    q = q // dims[2]
    b = q % dims[1]
    return (q // dims[1], b, c, d)


def starts_of(sel):
    return tuple(s.start for s in spans(sel))


def moved(base, ix):
    return tuple(s + i for s, i in zip(base, ix))


def count(dims):
    return dims[0] * dims[1] * dims[2] * dims[3]


def unit_slope(preact):
    sigma = 1.0 / (1.0 + jnp.exp(-preact))
    return sigma * (1.0 + preact * (1.0 - sigma))


def step_kernel(
    root_width, root_units,
    hid, cot, gain_in, lens_in, rew_in, swp_in, up, dn,
    out, new_up, new_dn, g_norm, g_out,
    h_rows, c_rows, out_rows, in_rows, meta, out_meta, in_meta, squares, packed, masks,
    w_up, w_dn, stream, acc, hidden, turned, slope, part,
    own_up, oth_up, got_up, own_dn, oth_dn, got_dn, tokens,
    relay_up, relay_dn, wide, gain, lens, rew, swp, *more
):
    half_bufs, full_bufs, two_bufs, one_bufs = (more[CHUNKS * n : CHUNKS * (n + 1)] for n in range(4))
    (
        sq_send, sq_recv, swap_send, swap_recv, meta_send, meta_recv,
        wy_send, wy_recv, wz_send, wz_recv, local_sem, core_send, core_recv,
        s1_send, s1_recv, s2_send, s2_recv, s3_send, s3_recv,
        stream_sem, gu_send, gu_recv, gd_send, gd_recv, nu_sem, nd_sem,
        h_send, h_recv, f_send, f_recv, t_send, t_recv, o_send, o_recv,
    ) = more[4 * CHUNKS :]
    at = place()
    row_count, slot_len, width = hid.shape
    units = 128
    f32, bf16 = jnp.float32, jnp.bfloat16

    loads = [
        pltpu.make_async_copy(src, dst, local_sem.at[4 + n])
        for n, (src, dst) in enumerate((
            (swp_in, swp), (hid, h_rows), (cot, c_rows), (lens_in, lens), (rew_in, rew), (gain_in, gain)
        ))
    ]
    for copy in loads:
        copy.start()
    mp_peers = [
        {**shifted(at, "y", dy), "z": (at["z"] // 2) * 2 + (at["z"] % 2 + dz) % 2}
        for dy in range(4) for dz in range(2) if dy or dz
    ]
    diagonal = [p for n, p in enumerate(mp_peers) if n in (2, 4, 6)]
    core = shifted(at, "c", 1)
    peers = axis_peers(at) + diagonal + [core]
    knock(peers)
    partners = (core, shifted(at, "z", 2), {**at, "x": (at["x"] // 2) * 2 + 1 - at["x"] % 2})

    store = (h_rows, c_rows)

    def swap_pick(r, a):
        out_rows[r, a, 0] = store[a][swp[0, r, 0]]
        out_rows[r, a, 1] = store[a][swp[0, r, 1]]

    def swap_start(r, a):
        if r:
            swap_pick(r, a)
        copy = remote(
            out_rows.at[r, a], in_rows.at[r, a], swap_send.at[r, a], swap_recv.at[r, a], partners[r]
        )
        copy.start()
        return copy

    def swap_end(r, a, copy):
        copy.wait()
        first, second = swp[0, r, 0], swp[0, r, 1]
        for s in range(row_count):
            store[a][s] = jnp.where(
                first == s, in_rows[r, a, 0], jnp.where(second == s, in_rows[r, a, 1], store[a][s])
            )

    def meta_start(r):
        out_meta[r, 0] = meta[swp[0, r, 0]]
        out_meta[r, 1] = meta[swp[0, r, 1]]
        copy = remote(out_meta.at[r], in_meta.at[r], meta_send.at[r], meta_recv.at[r], partners[r])
        copy.start()
        return copy

    def meta_end(r, copy):
        copy.wait()
        first, second = swp[0, r, 0], swp[0, r, 1]
        for s in range(row_count):
            meta[s] = jnp.where(first == s, in_meta[r, 0], jnp.where(second == s, in_meta[r, 1], meta[s]))

    def units_of(y, z_lo):
        return pl.ds(pl.multiple_of((y * 2 + z_lo) * units, units), units)

    z_lo = at["z"] % 2
    beside = {**at, "z": at["z"] + 1 - 2 * z_lo}
    own_units = pl.ds(pl.multiple_of(at["c"] * units, units), units)

    def weights_along_y():
        copies = {}
        for dy in (1, 3, 2):
            peer = shifted(at, "y", dy)
            near, far = units_of(peer["y"], z_lo), units_of(peer["y"], 1 - z_lo)
            moves = (
                (2, up.at[:, far], relay_up.at[at["y"]]),
                (3, dn.at[far], relay_dn.at[at["y"]]),
                (0, up.at[:, near], w_up.at[at["y"], z_lo, :, own_units]),
                (1, dn.at[near], w_dn.at[at["y"], z_lo, own_units]),
            )
            for n, src, dst in moves:
                copy = remote(src, dst, wy_send.at[dy - 1, n], wy_recv.at[dy - 1, n], peer)
                copy.start()
                copies[dy, n] = copy
        near = units_of(at["y"], z_lo)
        for n, (src, dst) in enumerate(
            ((up.at[:, near], w_up.at[at["y"], z_lo, :, own_units]), (dn.at[near], w_dn.at[at["y"], z_lo, own_units]))
        ):
            copies[0, n] = pltpu.make_async_copy(src, dst, local_sem.at[n])
            copies[0, n].start()
        return copies

    def weights_along_z(dy):
        y = (at["y"] - dy) % 4
        far = units_of(y, 1 - z_lo)
        from_up = relay_up.at[y] if dy else up.at[:, far]
        from_dn = relay_dn.at[y] if dy else dn.at[far]
        copies = [
            remote(from_up, w_up.at[y, z_lo, :, own_units], wz_send.at[dy, 0], wz_recv.at[dy, 0], beside),
            remote(from_dn, w_dn.at[y, z_lo, own_units], wz_send.at[dy, 1], wz_recv.at[dy, 1], beside),
        ]
        for copy in copies:
            copy.start()
        return copies

    def weights_to_core(n, which):
        copies = [
            remote(
                w_up.at[:, which, :, own_units], w_up.at[:, which, :, own_units],
                core_send.at[n, 0], core_recv.at[n, 0], core,
            ),
            remote(
                w_dn.at[:, which, own_units], w_dn.at[:, which, own_units],
                core_send.at[n, 1], core_recv.at[n, 1], core,
            ),
        ]
        for copy in copies:
            copy.start()
        return copies

    for copy in loads:
        copy.wait()
    swap_pick(0, 0)
    swap_pick(0, 1)
    flat = h_rows[...].reshape(row_count * slot_len, width).astype(f32)
    squares[7] = lax.dot_general(
        jnp.ones((8, width), f32), flat * flat, (((1,), (1,)), ((), ())),
        precision=lax.Precision.HIGHEST, preferred_element_type=f32,
    )
    enter(peers)
    move_h = swap_start(0, 0)
    move_c = swap_start(0, 1)
    sq_copies = []
    for n, peer in enumerate(mp_peers):
        copy = remote(squares.at[7], squares.at[n], sq_send.at[n], sq_recv.at[n], peer)
        copy.start()
        sq_copies.append(copy)
    y_copies = weights_along_y()
    swap_end(0, 0, move_h)
    move_h = swap_start(1, 0)
    total = squares[7]
    for n, copy in enumerate(sq_copies):
        copy.wait()
        total = total + squares[n]
    factor = lax.rsqrt(total / (8 * width) + norm_eps)
    for s in range(row_count):
        meta[s, 0:1] = jnp.full((1, 128), lens[s].astype(f32), f32)
        meta[s, 1:2] = jnp.full((1, 128), rew[s].astype(f32), f32)
        meta[s, 2:8] = jnp.zeros((6, 128), f32)
        meta[s, 2:3, 0:slot_len] = factor[0:1, s * slot_len : (s + 1) * slot_len]
    move_m = meta_start(0)
    swap_end(0, 1, move_c)
    meta_end(0, move_m)
    move_m = meta_start(1)
    move_c = swap_start(1, 1)
    z_copies = weights_along_z(0)
    swap_end(1, 0, move_h)
    move_h = swap_start(2, 0)
    meta_end(1, move_m)
    move_m = meta_start(2)
    swap_end(1, 1, move_c)
    move_c = swap_start(2, 1)
    meta_end(2, move_m)
    norm_scale = jnp.zeros((CAP, 1), f32)
    grad_scale = jnp.zeros((CAP, 1), f32)
    for s in range(row_count):
        hit = row_mask(meta, s, slot_len)
        masks[s] = jnp.where(hit, 1.0, 0.0).astype(bf16)
        norm_scale += jnp.sum(jnp.where(hit, meta[s, 2:3, 0:slot_len], 0.0), axis=1, keepdims=True)
        grad_scale += jnp.sum(jnp.where(hit, meta[s, 1:2, 0:slot_len], 0.0), axis=1, keepdims=True)

    def pack(a):
        picked = jnp.zeros((CAP, width), f32)
        for s in range(row_count):
            picked = picked + jnp.dot(masks[s], store[a][s], preferred_element_type=f32)
        return picked

    here = spans({k: at[k] for k in "xyz"})
    bufs = (g_norm, g_out)
    own, first_copies, second_copies, third_copies = [], {}, {}, {}

    def gather_first(a):
        copy = pltpu.make_async_copy(packed.at[a], bufs[a].at[here], local_sem.at[2 + a])
        copy.start()
        own.append(copy)
        for n, (p, r0, nr, c0, nc) in enumerate(PARTS[a]):
            for k, step in enumerate(OFFSETS):
                spot = (pl.ds(r0, nr), pl.ds(c0, nc))
                copy = remote(
                    packed.at[(a,) + (slice(None),) * 4 + spot], bufs[a].at[here + spot],
                    s1_send.at[a, n, k], s1_recv.at[a, n, k], shifted(at, ORDERS[p][0], step),
                )
                copy.start()
                first_copies[a, n, k] = copy

    def gather_second(a):
        own[a].wait()
        for n, (p, r0, nr, c0, nc) in enumerate(PARTS[a]):
            for k in range(3):
                first_copies[a, n, k].wait()
            one, two, three = ORDERS[p]
            spot = (pl.ds(r0, nr), pl.ds(c0, nc))
            piece = bufs[a].at[spans({one: None, two: at[two], three: at[three]}) + spot]
            for k, step in enumerate(OFFSETS):
                copy = remote(
                    piece, piece, s2_send.at[a, n, k], s2_recv.at[a, n, k], shifted(at, two, step)
                )
                copy.start()
                second_copies[a, n, k] = copy

    def gather_third(a, n):
        p, r0, nr, c0, nc = PARTS[a][n]
        for k in range(3):
            second_copies[a, n, k].wait()
        one, two, three = ORDERS[p]
        spot = (pl.ds(r0, nr), pl.ds(c0, nc))
        piece = bufs[a].at[spans({one: None, two: None, three: at[three]}) + spot]
        for k, step in enumerate((1, 3)):
            copy = remote(
                piece, piece, s3_send.at[a, n, k], s3_recv.at[a, n, k], shifted(at, three, step)
            )
            copy.start()
            third_copies[a, n, k] = copy

    def gather_pass_on(a, n):
        p, r0, nr, c0, nc = PARTS[a][n]
        one, two, three = ORDERS[p]
        spot = (pl.ds(r0, nr), pl.ds(c0, nc))
        for k, step in enumerate((1, 3)):
            third_copies[a, n, k].wait()
            origin = (at[three] - step) % 4
            piece = bufs[a].at[spans({one: ("half", k), two: None, three: origin}) + spot]
            copy = remote(
                piece, piece, s3_send.at[a, n, 2 + k], s3_recv.at[a, n, 2 + k], shifted(at, three, step)
            )
            copy.start()
            third_copies[a, n, 2 + k] = copy

    def gather_end(a):
        for n in range(len(PARTS[a])):
            for k in range(2):
                third_copies[a, n, 2 + k].wait()

    swap_end(2, 0, move_h)
    packed[0, 0, 0, 0, 0] = (pack(0) * norm_scale * gain[...].reshape(1, width)).astype(bf16)
    gather_first(0)
    swap_end(2, 1, move_c)
    packed[1, 0, 0, 0, 0] = (pack(1) * (grad_scale / 4.0)).astype(bf16)
    gather_first(1)
    for dy in (1, 3):
        for n in (2, 3):
            y_copies[dy, n].wait()
        z_copies += weights_along_z(dy)
    gather_second(0)
    for n in (2, 3):
        y_copies[2, n].wait()
    z_copies += weights_along_z(2)
    gather_second(1)
    for n in range(len(PARTS[0])):
        gather_third(0, n)
    for dy in range(4):
        for n in range(2):
            y_copies[dy, n].wait()
    core_copies = weights_to_core(0, z_lo)
    for n in range(len(PARTS[0])):
        gather_pass_on(0, n)
    for n in range(len(PARTS[1])):
        gather_third(1, n)
    for copy in z_copies:
        copy.wait()
    core_copies += weights_to_core(1, 1 - z_lo)
    gather_end(0)
    for copy in core_copies:
        copy.wait()

    tokens_here = 8 * CAP

    def streamed(buf, body):
        def fetch(j, slot):
            return pltpu.make_async_copy(buf.at[j // 2, j % 2], stream.at[slot], stream_sem.at[slot])

        fetch(0, 0).start()

        def turn(j, carry):
            slot = j % 2

            @pl.when(j < 7)
            def _():
                fetch(j + 1, 1 - slot).start()

            fetch(j, slot).wait()
            body(j, stream[slot].reshape(tokens_here, width))
            return carry

        lax.fori_loop(0, 8, turn, 0)

    rows_x = 2 * CAP

    def fetch_x(x, slot):
        return pltpu.make_async_copy(g_norm.at[:, :, x], wide.at[slot], stream_sem.at[slot])

    fetch_x(0, 0).start()

    def forward(x, carry):
        slot = x % 2

        @pl.when(x < 3)
        def _():
            fetch_x(x + 1, 1 - slot).start()

        fetch_x(x, slot).wait()
        value = jnp.zeros((rows_x, 256), f32)
        for j in range(8):
            value = value + jnp.dot(
                wide[slot, j // 2, j % 2].reshape(rows_x, width), w_up[j // 2, j % 2],
                preferred_element_type=f32,
            )
        value = value / root_width
        sigma = 1.0 / (1.0 + jnp.exp(-value))
        here_x = pl.ds(pl.multiple_of(x * rows_x, rows_x), rows_x)
        slope[here_x] = sigma * (1.0 + value * (1.0 - sigma))
        hidden[here_x] = (value * sigma).astype(bf16)
        return carry

    lax.fori_loop(0, 4, forward, 0)
    for n in range(len(PARTS[1])):
        gather_pass_on(1, n)

    def down(j, carry):
        block = jnp.dot(hidden[...], w_dn[j // 2, j % 2], preferred_element_type=f32)
        part[j // 2, j % 2] = block.astype(bf16).reshape(4, 2, CAP, width)
        return carry

    lax.fori_loop(0, 8, down, 0)

    sends = {}
    for n, (p, r0, nr, c0, nc) in enumerate(PARTS[2]):
        one, two, three = ORDERS[p]
        spot = (pl.ds(r0, nr), pl.ds(c0, nc))
        for k, step in enumerate((1, 3)):
            src = part.at[spans({one: (at[one] + 2) % 4, two: ("half", k), three: None}) + spot]
            sends[n, k] = remote(
                src, half_bufs[n].at[k], h_send.at[n, k], h_recv.at[n, k], shifted(at, one, step)
            )
            sends[n, k].start()
    for n, (p, r0, nr, c0, nc) in enumerate(PARTS[2]):
        one, two, three = ORDERS[p]
        spot = (pl.ds(r0, nr), pl.ds(c0, nc))
        for k, step in enumerate((1, 3)):
            other = 1 - k
            src = part.at[spans({one: (at[one] + step) % 4, two: ("half", other), three: None}) + spot]
            dst = full_bufs[n].at[(k,) + spans({one: 0, two: ("half", other), three: None})]
            sends[n, 2 + k] = remote(
                src, dst, f_send.at[n, k, 0], f_recv.at[n, k, 0], shifted(at, one, step)
            )
            sends[n, 2 + k].start()

    gather_end(1)
    acc[...] = jnp.zeros_like(acc)
    turned[...] = jnp.transpose(hidden[...])
    own_first = at["c"] == 0
    own_rows = pl.ds(pl.multiple_of(at["c"] * units, units), units)

    def give(buf, dst, send, recv, j):
        return remote(buf.at[j], dst.at[j], send.at[j], recv.at[j], core)

    def backward(j, block):
        acc[...] += lax.dot_general(block, w_dn[j // 2, j % 2], (((1,), (1,)), ((), ())), preferred_element_type=f32)
        grad = jnp.dot(turned[...], block, preferred_element_type=f32) * (step_size / root_units)
        low, high = grad[:units], grad[units:]
        own_dn[j] = w_dn[j // 2, j % 2, own_rows].astype(f32) - jnp.where(own_first, low, high)
        oth_dn[j] = jnp.where(own_first, high, low)
        give(oth_dn, got_dn, gd_send, gd_recv, j).start()

    streamed(g_out, backward)

    for n, (p, r0, nr, c0, nc) in enumerate(PARTS[2]):
        one, two, three = ORDERS[p]
        spot = (pl.ds(r0, nr), pl.ds(c0, nc))
        for k, step in enumerate((1, 3)):
            sends[n, k].wait()
            sel = {one: 0, two: ("half", k), three: None}
            dims = sizes(sel, nr, nc)[:4]
            base = starts_of({one: (at[one] + step) % 4, two: ("half", k), three: None})

            def add(q, carry, n=n, k=k, dims=dims, base=base, spot=spot):
                ix = lead(q, dims)
                half_bufs[n][(k,) + ix] = half_bufs[n][(k,) + ix] + part[moved(base, ix) + spot]
                return carry

            lax.fori_loop(0, count(dims), add, 0)
            dst = full_bufs[n].at[(k,) + spans(sel)]
            sends[n, 4 + k] = remote(
                half_bufs[n].at[k], dst, f_send.at[n, k, 1], f_recv.at[n, k, 1], shifted(at, one, step)
            )
            sends[n, 4 + k].start()

    turned[...] = jnp.transpose((acc[...] / root_units * slope[...]).astype(bf16))

    def up_grad(j, block):
        grad = jnp.dot(turned[...], block, preferred_element_type=f32) * (step_size / root_width)
        low, high = jnp.transpose(grad[:units]), jnp.transpose(grad[units:])
        weight = w_up[j // 2, j % 2].astype(f32)
        base = jnp.where(own_first, weight[:, :units], weight[:, units:])
        own_up[j] = base - jnp.where(own_first, low, high)
        oth_up[j] = jnp.where(own_first, high, low)
        give(oth_up, got_up, gu_send, gu_recv, j).start()

    streamed(g_norm, up_grad)

    def put_dn(j):
        return pltpu.make_async_copy(
            own_dn.at[j], new_dn.at[:, pl.ds(pl.multiple_of(j * width, 128), width)], nd_sem.at[j]
        )

    def put_up(j):
        return pltpu.make_async_copy(
            own_up.at[j], new_up.at[pl.ds(pl.multiple_of(j * width, 128), width)], nu_sem.at[j]
        )

    def finish_dn(j, carry):
        give(oth_dn, got_dn, gd_send, gd_recv, j).wait()
        own_dn[j] = own_dn[j] - got_dn[j]
        put_dn(j).start()
        return carry

    def finish_up(j, carry):
        give(oth_up, got_up, gu_send, gu_recv, j).wait()
        own_up[j] = own_up[j] - got_up[j]
        put_up(j).start()
        return carry

    lax.fori_loop(0, 8, finish_dn, 0)
    lax.fori_loop(0, 8, finish_up, 0)

    for n, (p, r0, nr, c0, nc) in enumerate(PARTS[2]):
        one, two, three = ORDERS[p]
        spot = (pl.ds(r0, nr), pl.ds(c0, nc))
        for m in (2, 3, 4, 5):
            sends[n, m].wait()
        for k, step in enumerate(OFFSETS + (0,)):
            index = (at[two] + step) % 4
            dims = sizes({one: 0, two: 0, three: None}, nr, nc)[:4]
            local = starts_of({one: 0, two: index, three: None})
            base = starts_of({one: at[one], two: index, three: None})

            def add(q, carry, n=n, dims=dims, local=local, base=base, spot=spot):
                ix = lead(q, dims)
                there = moved(local, ix)
                value = full_bufs[n][(0,) + there].astype(f32) + full_bufs[n][(1,) + there].astype(f32)
                value = value + part[moved(base, ix) + spot].astype(f32)
                full_bufs[n][(0,) + there] = value.astype(bf16)
                return carry

            lax.fori_loop(0, 4, add, 0)
            if step:
                src = full_bufs[n].at[(0,) + spans({one: 0, two: index, three: None})]
                sends[n, 6 + k] = remote(
                    src, two_bufs[n].at[k], t_send.at[n, k], t_recv.at[n, k], shifted(at, two, step)
                )
                sends[n, 6 + k].start()
    for n, (p, r0, nr, c0, nc) in enumerate(PARTS[2]):
        one, two, three = ORDERS[p]
        for k in range(3):
            sends[n, 6 + k].wait()
        dims = sizes({one: 0, two: 0, three: None}, nr, nc)[:4]
        local = starts_of({one: 0, two: at[two], three: None})
        for q in range(4):
            ix = lead(q, dims)
            value = full_bufs[n][(0,) + moved(local, ix)].astype(f32)
            for k in range(3):
                value = value + two_bufs[n][(k,) + ix].astype(f32)
            two_bufs[n][(0,) + ix] = value.astype(bf16)
        for k, step in enumerate(OFFSETS):
            src = two_bufs[n].at[(0,) + spans({one: 0, two: 0, three: (at[three] + step) % 4})]
            sends[n, 9 + k] = remote(
                src, one_bufs[n].at[k], o_send.at[n, k], o_recv.at[n, k], shifted(at, three, step)
            )
            sends[n, 9 + k].start()
    for n, (p, r0, nr, c0, nc) in enumerate(PARTS[2]):
        one, two, three = ORDERS[p]
        for k in range(3):
            sends[n, 9 + k].wait()
        there = starts_of({one: 0, two: 0, three: at[three]})
        value = two_bufs[n][(0,) + there].astype(f32)
        for k in range(3):
            value = value + one_bufs[n][k, 0, 0, 0, 0].astype(f32)
        tokens[pl.ds(r0, nr), pl.ds(c0, nc)] = (value / root_units).astype(bf16)
    for s in range(row_count):
        out[s] = lax.dot_general(
            masks[s], tokens[...], (((0,), (0,)), ((), ())), preferred_element_type=f32
        ).astype(bf16)

    def drain(j, carry):
        put_dn(j).wait()
        put_up(j).wait()
        return carry

    lax.fori_loop(0, 8, drain, 0)


def on_device(
    hidden_rows, cotangent, lengths, rewards, swap_rows, norm_gain, up_weight, down_weight
):
    row_count, slot_len, width = hidden_rows.shape
    root_width = math.sqrt(width * lax.axis_size("mp"))
    root_units = math.sqrt(up_weight.shape[1] * lax.axis_size("dp"))
    f32, bf16 = jnp.float32, jnp.bfloat16
    blocks = (4, 2, 4, 2, CAP, width)
    tokens = 8 * CAP
    dma = pltpu.SemaphoreType.DMA
    vmem = pl.BlockSpec(memory_space=pltpu.VMEM)
    hbm = pl.BlockSpec(memory_space=pl.ANY)
    half, full, two_b, one_b = [], [], [], []
    for p, _, nr, _, nc in PARTS[2]:
        one, two, three = ORDERS[p]
        half.append(pltpu.VMEM((2,) + sizes({one: 0, two: ("half", 0), three: None}, nr, nc), bf16))
        full.append(pltpu.VMEM((2,) + sizes({one: 0, two: None, three: None}, nr, nc), bf16))
        two_b.append(pltpu.VMEM((3,) + sizes({one: 0, two: 0, three: None}, nr, nc), bf16))
        one_b.append(pltpu.VMEM((3, 1, 1, 1, 1, nr, nc), bf16))

    def body(*refs):
        step_kernel(root_width, root_units, *refs)

    block_out, new_up, new_dn, _, _ = pl.pallas_call(
        body,
        out_shape=(
            jax.ShapeDtypeStruct((row_count, slot_len, width), bf16),
            jax.ShapeDtypeStruct((8 * width, 128), f32),
            jax.ShapeDtypeStruct((128, 8 * width), f32),
            jax.ShapeDtypeStruct(blocks, bf16),
            jax.ShapeDtypeStruct(blocks, bf16),
        ),
        in_specs=[hbm] * 8,
        out_specs=(vmem, hbm, hbm, hbm, hbm),
        scratch_shapes=[
            pltpu.VMEM((row_count, slot_len, width), bf16),
            pltpu.VMEM((row_count, slot_len, width), bf16),
            pltpu.VMEM((3, 2, 2, slot_len, width), bf16),
            pltpu.VMEM((3, 2, 2, slot_len, width), bf16),
            pltpu.VMEM((row_count, 8, 128), f32),
            pltpu.VMEM((3, 2, 8, 128), f32),
            pltpu.VMEM((3, 2, 8, 128), f32),
            pltpu.VMEM((8, 8, row_count * slot_len), f32),
            pltpu.VMEM((2, 1, 1, 1, 1, CAP, width), bf16),
            pltpu.VMEM((row_count, CAP, slot_len), bf16),
            pltpu.VMEM((4, 2, width, 256), bf16),
            pltpu.VMEM((4, 2, 256, width), bf16),
            pltpu.VMEM((2, 4, 2, CAP, width), bf16),
            pltpu.VMEM((tokens, 256), f32),
            pltpu.VMEM((tokens, 256), bf16),
            pltpu.VMEM((256, tokens), bf16),
            pltpu.VMEM((tokens, 256), f32),
            pltpu.VMEM(blocks, bf16),
            pltpu.VMEM((8, width, 128), f32),
            pltpu.VMEM((8, width, 128), f32),
            pltpu.VMEM((8, width, 128), f32),
            pltpu.VMEM((8, 128, width), f32),
            pltpu.VMEM((8, 128, width), f32),
            pltpu.VMEM((8, 128, width), f32),
            pltpu.VMEM((CAP, width), bf16),
            pltpu.VMEM((4, width, 128), bf16),
            pltpu.VMEM((4, 128, width), bf16),
            pltpu.VMEM((2, 4, 2, 2, CAP, width), bf16),
            pltpu.VMEM((width,), f32),
            pltpu.SMEM((row_count,), jnp.int32),
            pltpu.SMEM((row_count,), jnp.int32),
            pltpu.SMEM((1, 3, 2), jnp.int32),
        ] + half + full + two_b + one_b + [
            dma((7,)), dma((7,)), dma((3, 2)), dma((3, 2)), dma((3,)), dma((3,)),
            dma((3, 4)), dma((3, 4)), dma((4, 2)), dma((4, 2)), dma((10,)), dma((2, 2)), dma((2, 2)),
            dma((2, MOST, 3)), dma((2, MOST, 3)), dma((2, MOST, 3)), dma((2, MOST, 3)),
            dma((2, MOST, 4)), dma((2, MOST, 4)),
            dma((2,)), dma((8,)), dma((8,)), dma((8,)), dma((8,)), dma((8,)), dma((8,)),
            dma((CHUNKS, 2)), dma((CHUNKS, 2)), dma((CHUNKS, 2, 2)), dma((CHUNKS, 2, 2)),
            dma((CHUNKS, 3)), dma((CHUNKS, 3)), dma((CHUNKS, 3)), dma((CHUNKS, 3)),
        ],
        compiler_params=pltpu.CompilerParams(
            collective_id=1, has_side_effects=True, vmem_limit_bytes=60 << 20
        ),
        name="policy_step",
    )(
        hidden_rows, cotangent, norm_gain, lengths, rewards, swap_rows, up_weight, down_weight,
    )
    return (block_out, new_up, new_dn)


def solution(mesh):
    return jax.shard_map(
        on_device,
        mesh=mesh,
        in_specs=(
            P("dp", None, "mp"),
            P("dp", None, "mp"),
            P("dp"),
            P("dp"),
            P("dp", None, None),
            P("mp"),
            P("mp", "dp"),
            P("dp", "mp"),
        ),
        out_specs=(P("dp", None, "mp"), P(None, ("dp", "mp")), P(("dp", "mp"), None)),
        check_vma=False,
    )
```

```python
import math

import jax
import jax.numpy as jnp
from jax import lax
from jax.experimental import pallas as pl
from jax.experimental.pallas import tpu as pltpu
from jax.sharding import PartitionSpec as P

norm_eps = 1e-06
step_size = 4.0
MESH = pl.DeviceIdType.MESH

CAP = 128
ORDERS = (("x", "y", "z"), ("y", "z", "x"), ("z", "x", "y"))


def cut_block(last, *columns):
    chunks = []
    for c0, nc, rows in columns:
        r0 = 0
        for axis, nr in zip("xyz", rows):
            chunks.append((last[axis], r0, nr, c0, nc))
            r0 += nr
    return tuple(chunks)


GATHER_LAST = {"z": 0, "x": 1, "y": 2}
SCATTER_FIRST = {"x": 0, "y": 1, "z": 2}
PARTS = (
    cut_block(GATHER_LAST, (0, 640, (48, 48, 32))),
    cut_block(GATHER_LAST, (0, 384, (48, 32, 48)), (384, 256, (32, 48, 48))),
    cut_block(SCATTER_FIRST, (0, 384, (32, 48, 48)), (384, 256, (64, 32, 32))),
)
CHUNKS = len(PARTS[2])
MOST = max(len(chunks) for chunks in PARTS)
OFFSETS = (1, 3, 2)


def place():
    i = lax.axis_index("dp")
    j = lax.axis_index("mp")
    return {
        "x": i // 4,
        "y": j // 2,
        "z": ((i // 2) % 2) * 2 + j % 2,
        "c": i % 2,
    }


def device(at):
    z = at["z"]
    return ((at["x"] * 2 + z // 2) * 2 + at["c"], at["y"] * 2 + z % 2)


def shifted(at, axis, step):
    count = 2 if axis == "c" else 4
    return {**at, axis: (at[axis] + step) % count}


def spans(sel):
    def plain(s):
        if isinstance(s, tuple):
            return pl.ds(2 * s[1], 2)
        return pl.ds(0, 4) if s is None else pl.ds(s, 1)

    z = sel["z"]
    if z is None:
        z_lo, z_hi = pl.ds(0, 2), pl.ds(0, 2)
    elif isinstance(z, tuple):
        z_lo, z_hi = pl.ds(0, 2), pl.ds(z[1], 1)
    else:
        z_lo, z_hi = pl.ds(z % 2, 1), pl.ds(z // 2, 1)
    return (plain(sel["y"]), z_lo, plain(sel["x"]), z_hi)


def remote(src, dst, send, recv, at):
    return pltpu.make_async_remote_copy(
        src_ref=src,
        dst_ref=dst,
        send_sem=send,
        recv_sem=recv,
        device_id=device(at),
        device_id_type=MESH,
    )


def knock(peers):
    barrier = pltpu.get_barrier_semaphore()
    for at in peers:
        pl.semaphore_signal(barrier, inc=1, device_id=device(at), device_id_type=MESH)


def enter(peers):
    pl.semaphore_wait(pltpu.get_barrier_semaphore(), len(peers))


def axis_peers(at):
    return [shifted(at, axis, k) for axis in "xyz" for k in OFFSETS]


def row_mask(meta, slot, slot_len):
    length = meta[slot, 0:1, 0:1]
    start = jnp.zeros((1, 1), jnp.float32)
    for before in range(slot):
        start = start + meta[before, 0:1, 0:1]
    token = lax.broadcasted_iota(jnp.int32, (CAP, slot_len), 0).astype(jnp.float32)
    spot = lax.broadcasted_iota(jnp.int32, (CAP, slot_len), 1).astype(jnp.float32)
    return jnp.logical_and(token == spot + start, spot < length)


def sizes(sel, nr, width):
    def plain(s):
        return 2 if isinstance(s, tuple) else (4 if s is None else 1)

    z = sel["z"]
    z_dims = (2, 2) if z is None else ((2, 1) if isinstance(z, tuple) else (1, 1))
    return (plain(sel["y"]), z_dims[0], plain(sel["x"]), z_dims[1], nr, width)


def lead(q, dims):
    d = q % dims[3]
    q = q // dims[3]
    c = q % dims[2]
    q = q // dims[2]
    b = q % dims[1]
    return (q // dims[1], b, c, d)


def starts_of(sel):
    return tuple(s.start for s in spans(sel))


def moved(base, ix):
    return tuple(s + i for s, i in zip(base, ix))


def count(dims):
    return dims[0] * dims[1] * dims[2] * dims[3]


def unit_slope(preact):
    sigma = 1.0 / (1.0 + jnp.exp(-preact))
    return sigma * (1.0 + preact * (1.0 - sigma))


def step_kernel(
    root_width, root_units,
    hid, cot, gain_in, lens_in, rew_in, swp_in, up, dn,
    out, new_up, new_dn, g_norm, g_out,
    h_rows, c_rows, out_rows, in_rows, meta, out_meta, in_meta, squares, packed, masks,
    w_up, w_dn, stream, acc, hidden, turned, slope, part,
    own_up, oth_up, got_up, own_dn, oth_dn, got_dn, tokens,
    relay_up, relay_dn, wide, gain, lens, rew, swp, *more
):
    half_bufs, full_bufs, two_bufs, one_bufs = (more[CHUNKS * n : CHUNKS * (n + 1)] for n in range(4))
    (
        sq_send, sq_recv, swap_send, swap_recv, meta_send, meta_recv,
        wy_send, wy_recv, wz_send, wz_recv, local_sem, core_send, core_recv,
        s1_send, s1_recv, s2_send, s2_recv, s3_send, s3_recv,
        stream_sem, gu_send, gu_recv, gd_send, gd_recv, nu_sem, nd_sem,
        h_send, h_recv, f_send, f_recv, t_send, t_recv, o_send, o_recv,
    ) = more[4 * CHUNKS :]
    at = place()
    row_count, slot_len, width = hid.shape
    units = 128
    f32, bf16 = jnp.float32, jnp.bfloat16

    loads = [
        pltpu.make_async_copy(src, dst, local_sem.at[4 + n])
        for n, (src, dst) in enumerate((
            (swp_in, swp), (hid, h_rows), (cot, c_rows), (lens_in, lens), (rew_in, rew), (gain_in, gain)
        ))
    ]
    for copy in loads:
        copy.start()
    mp_peers = [
        {**shifted(at, "y", dy), "z": (at["z"] // 2) * 2 + (at["z"] % 2 + dz) % 2}
        for dy in range(4) for dz in range(2) if dy or dz
    ]
    diagonal = [p for n, p in enumerate(mp_peers) if n in (2, 4, 6)]
    core = shifted(at, "c", 1)
    peers = axis_peers(at) + diagonal + [core]
    knock(peers)
    partners = (core, shifted(at, "z", 2), {**at, "x": (at["x"] // 2) * 2 + 1 - at["x"] % 2})

    store = (h_rows, c_rows)

    def swap_pick(r, a):
        out_rows[r, a, 0] = store[a][swp[0, r, 0]]
        out_rows[r, a, 1] = store[a][swp[0, r, 1]]

    def swap_start(r, a):
        if r:
            swap_pick(r, a)
        copy = remote(
            out_rows.at[r, a], in_rows.at[r, a], swap_send.at[r, a], swap_recv.at[r, a], partners[r]
        )
        copy.start()
        return copy

    def swap_end(r, a, copy):
        copy.wait()
        first, second = swp[0, r, 0], swp[0, r, 1]
        for s in range(row_count):
            store[a][s] = jnp.where(
                first == s, in_rows[r, a, 0], jnp.where(second == s, in_rows[r, a, 1], store[a][s])
            )

    def meta_start(r):
        out_meta[r, 0] = meta[swp[0, r, 0]]
        out_meta[r, 1] = meta[swp[0, r, 1]]
        copy = remote(out_meta.at[r], in_meta.at[r], meta_send.at[r], meta_recv.at[r], partners[r])
        copy.start()
        return copy

    def meta_end(r, copy):
        copy.wait()
        first, second = swp[0, r, 0], swp[0, r, 1]
        for s in range(row_count):
            meta[s] = jnp.where(first == s, in_meta[r, 0], jnp.where(second == s, in_meta[r, 1], meta[s]))

    def units_of(y, z_lo):
        return pl.ds(pl.multiple_of((y * 2 + z_lo) * units, units), units)

    z_lo = at["z"] % 2
    beside = {**at, "z": at["z"] + 1 - 2 * z_lo}
    own_units = pl.ds(pl.multiple_of(at["c"] * units, units), units)

    def weights_along_y():
        copies = {}
        for dy in (1, 3, 2):
            peer = shifted(at, "y", dy)
            near, far = units_of(peer["y"], z_lo), units_of(peer["y"], 1 - z_lo)
            moves = (
                (2, up.at[:, far], relay_up.at[at["y"]]),
                (3, dn.at[far], relay_dn.at[at["y"]]),
                (0, up.at[:, near], w_up.at[at["y"], z_lo, :, own_units]),
                (1, dn.at[near], w_dn.at[at["y"], z_lo, own_units]),
            )
            for n, src, dst in moves:
                copy = remote(src, dst, wy_send.at[dy - 1, n], wy_recv.at[dy - 1, n], peer)
                copy.start()
                copies[dy, n] = copy
        near = units_of(at["y"], z_lo)
        for n, (src, dst) in enumerate(
            ((up.at[:, near], w_up.at[at["y"], z_lo, :, own_units]), (dn.at[near], w_dn.at[at["y"], z_lo, own_units]))
        ):
            copies[0, n] = pltpu.make_async_copy(src, dst, local_sem.at[n])
            copies[0, n].start()
        return copies

    def weights_along_z(dy):
        y = (at["y"] - dy) % 4
        far = units_of(y, 1 - z_lo)
        from_up = relay_up.at[y] if dy else up.at[:, far]
        from_dn = relay_dn.at[y] if dy else dn.at[far]
        copies = [
            remote(from_up, w_up.at[y, z_lo, :, own_units], wz_send.at[dy, 0], wz_recv.at[dy, 0], beside),
            remote(from_dn, w_dn.at[y, z_lo, own_units], wz_send.at[dy, 1], wz_recv.at[dy, 1], beside),
        ]
        for copy in copies:
            copy.start()
        return copies

    def weights_to_core(n, which):
        copies = [
            remote(
                w_up.at[:, which, :, own_units], w_up.at[:, which, :, own_units],
                core_send.at[n, 0], core_recv.at[n, 0], core,
            ),
            remote(
                w_dn.at[:, which, own_units], w_dn.at[:, which, own_units],
                core_send.at[n, 1], core_recv.at[n, 1], core,
            ),
        ]
        for copy in copies:
            copy.start()
        return copies

    for copy in loads:
        copy.wait()
    swap_pick(0, 0)
    swap_pick(0, 1)
    flat = h_rows[...].reshape(row_count * slot_len, width).astype(f32)
    squares[7] = lax.dot_general(
        jnp.ones((8, width), f32), flat * flat, (((1,), (1,)), ((), ())),
        precision=lax.Precision.HIGHEST, preferred_element_type=f32,
    )
    enter(peers)
    move_h = swap_start(0, 0)
    move_c = swap_start(0, 1)
    sq_copies = []
    for n, peer in enumerate(mp_peers):
        copy = remote(squares.at[7], squares.at[n], sq_send.at[n], sq_recv.at[n], peer)
        copy.start()
        sq_copies.append(copy)
    y_copies = weights_along_y()
    swap_end(0, 0, move_h)
    move_h = swap_start(1, 0)
    total = squares[7]
    for n, copy in enumerate(sq_copies):
        copy.wait()
        total = total + squares[n]
    factor = lax.rsqrt(total / (8 * width) + norm_eps)
    for s in range(row_count):
        meta[s, 0:1] = jnp.full((1, 128), lens[s].astype(f32), f32)
        meta[s, 1:2] = jnp.full((1, 128), rew[s].astype(f32), f32)
        meta[s, 2:8] = jnp.zeros((6, 128), f32)
        meta[s, 2:3, 0:slot_len] = factor[0:1, s * slot_len : (s + 1) * slot_len]
    move_m = meta_start(0)
    swap_end(0, 1, move_c)
    meta_end(0, move_m)
    move_m = meta_start(1)
    move_c = swap_start(1, 1)
    z_copies = weights_along_z(0)
    swap_end(1, 0, move_h)
    move_h = swap_start(2, 0)
    meta_end(1, move_m)
    move_m = meta_start(2)
    swap_end(1, 1, move_c)
    move_c = swap_start(2, 1)
    meta_end(2, move_m)
    norm_scale = jnp.zeros((CAP, 1), f32)
    grad_scale = jnp.zeros((CAP, 1), f32)
    for s in range(row_count):
        hit = row_mask(meta, s, slot_len)
        masks[s] = jnp.where(hit, 1.0, 0.0).astype(bf16)
        norm_scale += jnp.sum(jnp.where(hit, meta[s, 2:3, 0:slot_len], 0.0), axis=1, keepdims=True)
        grad_scale += jnp.sum(jnp.where(hit, meta[s, 1:2, 0:slot_len], 0.0), axis=1, keepdims=True)

    def pack(a):
        picked = jnp.zeros((CAP, width), f32)
        for s in range(row_count):
            picked = picked + jnp.dot(masks[s], store[a][s], preferred_element_type=f32)
        return picked

    here = spans({k: at[k] for k in "xyz"})
    bufs = (g_norm, g_out)
    own, first_copies, second_copies, third_copies = [], {}, {}, {}

    def gather_first(a):
        copy = pltpu.make_async_copy(packed.at[a], bufs[a].at[here], local_sem.at[2 + a])
        copy.start()
        own.append(copy)
        for n, (p, r0, nr, c0, nc) in enumerate(PARTS[a]):
            for k, step in enumerate(OFFSETS):
                spot = (pl.ds(r0, nr), pl.ds(c0, nc))
                copy = remote(
                    packed.at[(a,) + (slice(None),) * 4 + spot], bufs[a].at[here + spot],
                    s1_send.at[a, n, k], s1_recv.at[a, n, k], shifted(at, ORDERS[p][0], step),
                )
                copy.start()
                first_copies[a, n, k] = copy

    def gather_second(a):
        own[a].wait()
        for n, (p, r0, nr, c0, nc) in enumerate(PARTS[a]):
            for k in range(3):
                first_copies[a, n, k].wait()
            one, two, three = ORDERS[p]
            spot = (pl.ds(r0, nr), pl.ds(c0, nc))
            piece = bufs[a].at[spans({one: None, two: at[two], three: at[three]}) + spot]
            for k, step in enumerate(OFFSETS):
                copy = remote(
                    piece, piece, s2_send.at[a, n, k], s2_recv.at[a, n, k], shifted(at, two, step)
                )
                copy.start()
                second_copies[a, n, k] = copy

    def gather_third(a, n):
        p, r0, nr, c0, nc = PARTS[a][n]
        for k in range(3):
            second_copies[a, n, k].wait()
        one, two, three = ORDERS[p]
        spot = (pl.ds(r0, nr), pl.ds(c0, nc))
        piece = bufs[a].at[spans({one: None, two: None, three: at[three]}) + spot]
        for k, step in enumerate((1, 3)):
            copy = remote(
                piece, piece, s3_send.at[a, n, k], s3_recv.at[a, n, k], shifted(at, three, step)
            )
            copy.start()
            third_copies[a, n, k] = copy

    def gather_pass_on(a, n):
        p, r0, nr, c0, nc = PARTS[a][n]
        one, two, three = ORDERS[p]
        spot = (pl.ds(r0, nr), pl.ds(c0, nc))
        for k, step in enumerate((1, 3)):
            third_copies[a, n, k].wait()
            origin = (at[three] - step) % 4
            piece = bufs[a].at[spans({one: ("half", k), two: None, three: origin}) + spot]
            copy = remote(
                piece, piece, s3_send.at[a, n, 2 + k], s3_recv.at[a, n, 2 + k], shifted(at, three, step)
            )
            copy.start()
            third_copies[a, n, 2 + k] = copy

    def gather_end(a):
        for n in range(len(PARTS[a])):
            for k in range(2):
                third_copies[a, n, 2 + k].wait()

    swap_end(2, 0, move_h)
    packed[0, 0, 0, 0, 0] = (pack(0) * norm_scale * gain[...].reshape(1, width)).astype(bf16)
    gather_first(0)
    swap_end(2, 1, move_c)
    packed[1, 0, 0, 0, 0] = (pack(1) * (grad_scale / 4.0)).astype(bf16)
    gather_first(1)
    for dy in (1, 3):
        for n in (2, 3):
            y_copies[dy, n].wait()
        z_copies += weights_along_z(dy)
    gather_second(0)
    for n in (2, 3):
        y_copies[2, n].wait()
    z_copies += weights_along_z(2)
    gather_second(1)
    for n in range(len(PARTS[0])):
        gather_third(0, n)
    for dy in range(4):
        for n in range(2):
            y_copies[dy, n].wait()
    core_copies = weights_to_core(0, z_lo)
    for n in range(len(PARTS[0])):
        gather_pass_on(0, n)
    for n in range(len(PARTS[1])):
        gather_third(1, n)
    for copy in z_copies:
        copy.wait()
    core_copies += weights_to_core(1, 1 - z_lo)
    gather_end(0)
    for copy in core_copies:
        copy.wait()

    tokens_here = 8 * CAP

    def streamed(buf, body):
        def fetch(j, slot):
            return pltpu.make_async_copy(buf.at[j // 2, j % 2], stream.at[slot], stream_sem.at[slot])

        fetch(0, 0).start()

        def turn(j, carry):
            slot = j % 2

            @pl.when(j < 7)
            def _():
                fetch(j + 1, 1 - slot).start()

            fetch(j, slot).wait()
            body(j, stream[slot].reshape(tokens_here, width))
            return carry

        lax.fori_loop(0, 8, turn, 0)

    rows_x = 2 * CAP

    def fetch_x(x, slot):
        return pltpu.make_async_copy(g_norm.at[:, :, x], wide.at[slot], stream_sem.at[slot])

    fetch_x(0, 0).start()

    def forward(x, carry):
        slot = x % 2

        @pl.when(x < 3)
        def _():
            fetch_x(x + 1, 1 - slot).start()

        fetch_x(x, slot).wait()
        value = jnp.zeros((rows_x, 256), f32)
        for j in range(8):
            value = value + jnp.dot(
                wide[slot, j // 2, j % 2].reshape(rows_x, width), w_up[j // 2, j % 2],
                preferred_element_type=f32,
            )
        value = value / root_width
        sigma = 1.0 / (1.0 + jnp.exp(-value))
        here_x = pl.ds(pl.multiple_of(x * rows_x, rows_x), rows_x)
        slope[here_x] = sigma * (1.0 + value * (1.0 - sigma))
        hidden[here_x] = (value * sigma).astype(bf16)
        return carry

    lax.fori_loop(0, 4, forward, 0)
    for n in range(len(PARTS[1])):
        gather_pass_on(1, n)

    def down(j, carry):
        block = jnp.dot(hidden[...], w_dn[j // 2, j % 2], preferred_element_type=f32)
        part[j // 2, j % 2] = block.astype(bf16).reshape(4, 2, CAP, width)
        return carry

    lax.fori_loop(0, 8, down, 0)

    sends = {}
    for n, (p, r0, nr, c0, nc) in enumerate(PARTS[2]):
        one, two, three = ORDERS[p]
        spot = (pl.ds(r0, nr), pl.ds(c0, nc))
        for k, step in enumerate((1, 3)):
            src = part.at[spans({one: (at[one] + 2) % 4, two: ("half", k), three: None}) + spot]
            sends[n, k] = remote(
                src, half_bufs[n].at[k], h_send.at[n, k], h_recv.at[n, k], shifted(at, one, step)
            )
            sends[n, k].start()
    for n, (p, r0, nr, c0, nc) in enumerate(PARTS[2]):
        one, two, three = ORDERS[p]
        spot = (pl.ds(r0, nr), pl.ds(c0, nc))
        for k, step in enumerate((1, 3)):
            other = 1 - k
            src = part.at[spans({one: (at[one] + step) % 4, two: ("half", other), three: None}) + spot]
            dst = full_bufs[n].at[(k,) + spans({one: 0, two: ("half", other), three: None})]
            sends[n, 2 + k] = remote(
                src, dst, f_send.at[n, k, 0], f_recv.at[n, k, 0], shifted(at, one, step)
            )
            sends[n, 2 + k].start()

    gather_end(1)
    acc[...] = jnp.zeros_like(acc)
    turned[...] = jnp.transpose(hidden[...])
    own_first = at["c"] == 0
    own_rows = pl.ds(pl.multiple_of(at["c"] * units, units), units)

    def give(buf, dst, send, recv, j):
        return remote(buf.at[j], dst.at[j], send.at[j], recv.at[j], core)

    def backward(j, block):
        acc[...] += lax.dot_general(block, w_dn[j // 2, j % 2], (((1,), (1,)), ((), ())), preferred_element_type=f32)
        grad = jnp.dot(turned[...], block, preferred_element_type=f32) * (step_size / root_units)
        low, high = grad[:units], grad[units:]
        own_dn[j] = w_dn[j // 2, j % 2, own_rows].astype(f32) - jnp.where(own_first, low, high)
        oth_dn[j] = jnp.where(own_first, high, low)
        give(oth_dn, got_dn, gd_send, gd_recv, j).start()

    streamed(g_out, backward)

    for n, (p, r0, nr, c0, nc) in enumerate(PARTS[2]):
        one, two, three = ORDERS[p]
        spot = (pl.ds(r0, nr), pl.ds(c0, nc))
        for k, step in enumerate((1, 3)):
            sends[n, k].wait()
            sel = {one: 0, two: ("half", k), three: None}
            dims = sizes(sel, nr, nc)[:4]
            base = starts_of({one: (at[one] + step) % 4, two: ("half", k), three: None})

            def add(q, carry, n=n, k=k, dims=dims, base=base, spot=spot):
                ix = lead(q, dims)
                half_bufs[n][(k,) + ix] = half_bufs[n][(k,) + ix] + part[moved(base, ix) + spot]
                return carry

            lax.fori_loop(0, count(dims), add, 0)
            dst = full_bufs[n].at[(k,) + spans(sel)]
            sends[n, 4 + k] = remote(
                half_bufs[n].at[k], dst, f_send.at[n, k, 1], f_recv.at[n, k, 1], shifted(at, one, step)
            )
            sends[n, 4 + k].start()

    turned[...] = jnp.transpose((acc[...] / root_units * slope[...]).astype(bf16))

    def up_grad(j, block):
        grad = jnp.dot(turned[...], block, preferred_element_type=f32) * (step_size / root_width)
        low, high = jnp.transpose(grad[:units]), jnp.transpose(grad[units:])
        weight = w_up[j // 2, j % 2].astype(f32)
        base = jnp.where(own_first, weight[:, :units], weight[:, units:])
        own_up[j] = base - jnp.where(own_first, low, high)
        oth_up[j] = jnp.where(own_first, high, low)
        give(oth_up, got_up, gu_send, gu_recv, j).start()

    streamed(g_norm, up_grad)

    def put_dn(j):
        return pltpu.make_async_copy(
            own_dn.at[j], new_dn.at[:, pl.ds(pl.multiple_of(j * width, 128), width)], nd_sem.at[j]
        )

    def put_up(j):
        return pltpu.make_async_copy(
            own_up.at[j], new_up.at[pl.ds(pl.multiple_of(j * width, 128), width)], nu_sem.at[j]
        )

    def finish_dn(j, carry):
        give(oth_dn, got_dn, gd_send, gd_recv, j).wait()
        own_dn[j] = own_dn[j] - got_dn[j]
        put_dn(j).start()
        return carry

    def finish_up(j, carry):
        give(oth_up, got_up, gu_send, gu_recv, j).wait()
        own_up[j] = own_up[j] - got_up[j]
        put_up(j).start()
        return carry


    for n, (p, r0, nr, c0, nc) in enumerate(PARTS[2]):
        one, two, three = ORDERS[p]
        spot = (pl.ds(r0, nr), pl.ds(c0, nc))
        for m in (2, 3, 4, 5):
            sends[n, m].wait()
        for k, step in enumerate(OFFSETS + (0,)):
            index = (at[two] + step) % 4
            dims = sizes({one: 0, two: 0, three: None}, nr, nc)[:4]
            local = starts_of({one: 0, two: index, three: None})
            base = starts_of({one: at[one], two: index, three: None})

            def add(q, carry, n=n, dims=dims, local=local, base=base, spot=spot):
                ix = lead(q, dims)
                there = moved(local, ix)
                value = full_bufs[n][(0,) + there].astype(f32) + full_bufs[n][(1,) + there].astype(f32)
                value = value + part[moved(base, ix) + spot].astype(f32)
                full_bufs[n][(0,) + there] = value.astype(bf16)
                return carry

            lax.fori_loop(0, 4, add, 0)
            if step:
                src = full_bufs[n].at[(0,) + spans({one: 0, two: index, three: None})]
                sends[n, 6 + k] = remote(
                    src, two_bufs[n].at[k], t_send.at[n, k], t_recv.at[n, k], shifted(at, two, step)
                )
                sends[n, 6 + k].start()
    lax.fori_loop(0, 8, finish_dn, 0)
    lax.fori_loop(0, 8, finish_up, 0)
    for n, (p, r0, nr, c0, nc) in enumerate(PARTS[2]):
        one, two, three = ORDERS[p]
        for k in range(3):
            sends[n, 6 + k].wait()
        dims = sizes({one: 0, two: 0, three: None}, nr, nc)[:4]
        local = starts_of({one: 0, two: at[two], three: None})
        for q in range(4):
            ix = lead(q, dims)
            value = full_bufs[n][(0,) + moved(local, ix)].astype(f32)
            for k in range(3):
                value = value + two_bufs[n][(k,) + ix].astype(f32)
            two_bufs[n][(0,) + ix] = value.astype(bf16)
        for k, step in enumerate(OFFSETS):
            src = two_bufs[n].at[(0,) + spans({one: 0, two: 0, three: (at[three] + step) % 4})]
            sends[n, 9 + k] = remote(
                src, one_bufs[n].at[k], o_send.at[n, k], o_recv.at[n, k], shifted(at, three, step)
            )
            sends[n, 9 + k].start()
    for n, (p, r0, nr, c0, nc) in enumerate(PARTS[2]):
        one, two, three = ORDERS[p]
        for k in range(3):
            sends[n, 9 + k].wait()
        there = starts_of({one: 0, two: 0, three: at[three]})
        value = two_bufs[n][(0,) + there].astype(f32)
        for k in range(3):
            value = value + one_bufs[n][k, 0, 0, 0, 0].astype(f32)
        tokens[pl.ds(r0, nr), pl.ds(c0, nc)] = (value / root_units).astype(bf16)
    for s in range(row_count):
        out[s] = lax.dot_general(
            masks[s], tokens[...], (((0,), (0,)), ((), ())), preferred_element_type=f32
        ).astype(bf16)

    def drain(j, carry):
        put_dn(j).wait()
        put_up(j).wait()
        return carry

    lax.fori_loop(0, 8, drain, 0)


def on_device(
    hidden_rows, cotangent, lengths, rewards, swap_rows, norm_gain, up_weight, down_weight
):
    row_count, slot_len, width = hidden_rows.shape
    root_width = math.sqrt(width * lax.axis_size("mp"))
    root_units = math.sqrt(up_weight.shape[1] * lax.axis_size("dp"))
    f32, bf16 = jnp.float32, jnp.bfloat16
    blocks = (4, 2, 4, 2, CAP, width)
    tokens = 8 * CAP
    dma = pltpu.SemaphoreType.DMA
    vmem = pl.BlockSpec(memory_space=pltpu.VMEM)
    hbm = pl.BlockSpec(memory_space=pl.ANY)
    half, full, two_b, one_b = [], [], [], []
    for p, _, nr, _, nc in PARTS[2]:
        one, two, three = ORDERS[p]
        half.append(pltpu.VMEM((2,) + sizes({one: 0, two: ("half", 0), three: None}, nr, nc), bf16))
        full.append(pltpu.VMEM((2,) + sizes({one: 0, two: None, three: None}, nr, nc), bf16))
        two_b.append(pltpu.VMEM((3,) + sizes({one: 0, two: 0, three: None}, nr, nc), bf16))
        one_b.append(pltpu.VMEM((3, 1, 1, 1, 1, nr, nc), bf16))

    def body(*refs):
        step_kernel(root_width, root_units, *refs)

    block_out, new_up, new_dn, _, _ = pl.pallas_call(
        body,
        out_shape=(
            jax.ShapeDtypeStruct((row_count, slot_len, width), bf16),
            jax.ShapeDtypeStruct((8 * width, 128), f32),
            jax.ShapeDtypeStruct((128, 8 * width), f32),
            jax.ShapeDtypeStruct(blocks, bf16),
            jax.ShapeDtypeStruct(blocks, bf16),
        ),
        in_specs=[hbm] * 8,
        out_specs=(vmem, hbm, hbm, hbm, hbm),
        scratch_shapes=[
            pltpu.VMEM((row_count, slot_len, width), bf16),
            pltpu.VMEM((row_count, slot_len, width), bf16),
            pltpu.VMEM((3, 2, 2, slot_len, width), bf16),
            pltpu.VMEM((3, 2, 2, slot_len, width), bf16),
            pltpu.VMEM((row_count, 8, 128), f32),
            pltpu.VMEM((3, 2, 8, 128), f32),
            pltpu.VMEM((3, 2, 8, 128), f32),
            pltpu.VMEM((8, 8, row_count * slot_len), f32),
            pltpu.VMEM((2, 1, 1, 1, 1, CAP, width), bf16),
            pltpu.VMEM((row_count, CAP, slot_len), bf16),
            pltpu.VMEM((4, 2, width, 256), bf16),
            pltpu.VMEM((4, 2, 256, width), bf16),
            pltpu.VMEM((2, 4, 2, CAP, width), bf16),
            pltpu.VMEM((tokens, 256), f32),
            pltpu.VMEM((tokens, 256), bf16),
            pltpu.VMEM((256, tokens), bf16),
            pltpu.VMEM((tokens, 256), f32),
            pltpu.VMEM(blocks, bf16),
            pltpu.VMEM((8, width, 128), f32),
            pltpu.VMEM((8, width, 128), f32),
            pltpu.VMEM((8, width, 128), f32),
            pltpu.VMEM((8, 128, width), f32),
            pltpu.VMEM((8, 128, width), f32),
            pltpu.VMEM((8, 128, width), f32),
            pltpu.VMEM((CAP, width), bf16),
            pltpu.VMEM((4, width, 128), bf16),
            pltpu.VMEM((4, 128, width), bf16),
            pltpu.VMEM((2, 4, 2, 2, CAP, width), bf16),
            pltpu.VMEM((width,), f32),
            pltpu.SMEM((row_count,), jnp.int32),
            pltpu.SMEM((row_count,), jnp.int32),
            pltpu.SMEM((1, 3, 2), jnp.int32),
        ] + half + full + two_b + one_b + [
            dma((7,)), dma((7,)), dma((3, 2)), dma((3, 2)), dma((3,)), dma((3,)),
            dma((3, 4)), dma((3, 4)), dma((4, 2)), dma((4, 2)), dma((10,)), dma((2, 2)), dma((2, 2)),
            dma((2, MOST, 3)), dma((2, MOST, 3)), dma((2, MOST, 3)), dma((2, MOST, 3)),
            dma((2, MOST, 4)), dma((2, MOST, 4)),
            dma((2,)), dma((8,)), dma((8,)), dma((8,)), dma((8,)), dma((8,)), dma((8,)),
            dma((CHUNKS, 2)), dma((CHUNKS, 2)), dma((CHUNKS, 2, 2)), dma((CHUNKS, 2, 2)),
            dma((CHUNKS, 3)), dma((CHUNKS, 3)), dma((CHUNKS, 3)), dma((CHUNKS, 3)),
        ],
        compiler_params=pltpu.CompilerParams(
            collective_id=1, has_side_effects=True, vmem_limit_bytes=60 << 20
        ),
        name="policy_step",
    )(
        hidden_rows, cotangent, norm_gain, lengths, rewards, swap_rows, up_weight, down_weight,
    )
    return (block_out, new_up, new_dn)


def solution(mesh):
    return jax.shard_map(
        on_device,
        mesh=mesh,
        in_specs=(
            P("dp", None, "mp"),
            P("dp", None, "mp"),
            P("dp"),
            P("dp"),
            P("dp", None, None),
            P("mp"),
            P("mp", "dp"),
            P("dp", "mp"),
        ),
        out_specs=(P("dp", None, "mp"), P(None, ("dp", "mp")), P(("dp", "mp"), None)),
        check_vma=False,
    )
```
